256 devices in a mesh: wide: 64 (over x, y_hi, z), narrow: 4 (over y_lo, core).
Axes of the slice: x: 4, y: 4 (y_hi: 2, y_lo: 2; y = y_hi * 2 + y_lo), z: 8, core: 2. Of those that a mesh axis runs over, the one named last changes fastest.
Arguments:
- image_embed: float32 [16384, 1152], P(('wide', 'narrow')), as said below
- text_embed: float32 [16384, 1152], P(('wide', 'narrow')), as said below
- log_temp: float32 [1], replicated, may hold values from 2.3 to 3
- bias: float32 [1], replicated, may hold values from -11 to -9
Outputs:
- loss: float32 [1], replicated
- image_grad: float32 [16384, 1152], P(('wide', 'narrow'))
- text_grad: float32 [16384, 1152], P(('wide', 'narrow'))
- temp_grad: float32 [1], replicated
- bias_grad: float32 [1], replicated
The draws below stay inside these ranges and needn't reach their ends.
Inputs may be any that keep to these rules, and one draw needn't show every extreme that they name: `image_embed`: rows of real numbers whose lengths differ from row to row. `text_embed`: rows of real numbers whose lengths differ from row to row.
All inputs are finite; a program needn't handle non-finite values.
Results may differ from the reference program's by a relative error of at most 0.0018.
Values may be sent and summed in bfloat16 or wider, within the bound.
A program may use at most 128 MiB of HBM per device.

```python
import math
import jax
import jax.numpy as jnp
from jax import lax

D = 1152
ROWS_DEV = 64
TOKENS = 16384


def shared_part(key):
    first, second, third = jax.random.split(key, 3)
    groups = max(1, TOKENS // 64)
    group_ids = jax.random.randint(first, (TOKENS,), 0, groups)
    centers = jax.random.normal(second, (groups, D), jnp.float32)
    common = jax.random.normal(third, (TOKENS, D), jnp.float32)
    return (common, jnp.take(centers, group_ids, axis=0))


def row_scales(key):
    spread = jax.random.uniform(key, (TOKENS, 1), jnp.float32)
    return jnp.exp(spread * math.log(10.0)) / math.sqrt(D)


def draw_image_embed(key, part):
    common, grouped = shared_part(key)
    key = jax.random.fold_in(key, 11)
    first = jax.random.fold_in(key, 0)
    second = jax.random.fold_in(key, 1)
    fourth = jax.random.fold_in(key, 3)
    own = jax.random.normal(first, (TOKENS, D), jnp.float32)
    weight = jax.random.uniform(fourth, (TOKENS, 1), jnp.float32, 0.2, 1.2)
    base = weight * grouped + 0.8 * common + 0.5 * own
    return base * row_scales(second)


def draw_text_embed(key, part):
    common, grouped = shared_part(key)
    key = jax.random.fold_in(key, 23)
    first = jax.random.fold_in(key, 0)
    second = jax.random.fold_in(key, 1)
    fourth = jax.random.fold_in(key, 3)
    own = jax.random.normal(first, (TOKENS, D), jnp.float32)
    weight = jax.random.uniform(fourth, (TOKENS, 1), jnp.float32, 0.2, 1.2)
    base = weight * grouped + 0.7 * common + 0.6 * own
    return base * row_scales(second)


def setup_inputs(seed: int = 0) -> dict:
    key_of = jax.random.split(jax.random.key(seed), 5)
    return {
        "image_embed": draw_image_embed(jax.random.fold_in(key_of[4], 71), 0),
        "text_embed": draw_text_embed(jax.random.fold_in(key_of[4], 71), 0),
        "log_temp": jnp.clip(jax.random.uniform(key_of[2], (1,), jnp.float32, 2.3, 3.0), 2.3, 3.0),
        "bias": jnp.clip(jax.random.uniform(key_of[3], (1,), jnp.float32, -11.0, -9.0), -11.0, -9.0),
    }


EPS = 1e-06

def unit_rows(values):
    inverse = lax.rsqrt(lax.optimization_barrier(jnp.sum(values * values, axis=1, keepdims=True)) + EPS)
    return (values * inverse, inverse)

def back_rows(unit, inverse, direction):
    along = lax.optimization_barrier(jnp.sum(unit * direction, axis=1, keepdims=True))
    return inverse * (direction - unit * along)

def reference(image_embed, text_embed, log_temp, bias):
    total = image_embed.shape[0]
    width = image_embed.shape[1]
    image_unit, inv_image = unit_rows(image_embed)
    text_unit, inv_text = unit_rows(text_embed)
    image_low = image_unit.astype(jnp.bfloat16)
    text_low = text_unit.astype(jnp.bfloat16)
    scale = jnp.exp(log_temp[0])
    offset = bias[0]
    block = 4 * ROWS_DEV
    count = total // block
    columns = jnp.arange(total, dtype=jnp.int32)

    def step(carry, index):
        text_dir, loss_sum, temp_sum, bias_sum = carry
        start = (index * block).astype(jnp.int32)
        rows_low = lax.dynamic_slice_in_dim(image_low, start, block, 0)
        sim = lax.dot_general(rows_low, text_low, (((1,), (1,)), ((), ())), preferred_element_type=jnp.float32)
        logits = scale * sim + offset
        row_ids = start + jnp.arange(block, dtype=jnp.int32)
        label = jnp.where(row_ids[:, None] == columns[None, :], 1.0, -1.0).astype(logits.dtype)
        loss_sum = loss_sum + jnp.sum(jax.nn.softplus(-label * logits))
        pair_grad = -label * jax.nn.sigmoid(-label * logits)
        temp_sum = temp_sum + jnp.sum(pair_grad * scale * sim)
        bias_sum = bias_sum + jnp.sum(pair_grad)
        pair_low = pair_grad.astype(jnp.bfloat16)
        image_dir = scale * jnp.dot(pair_low, text_low, preferred_element_type=jnp.float32)
        text_dir = text_dir + scale * lax.dot_general(pair_low, rows_low, (((0,), (0,)), ((), ())), preferred_element_type=jnp.float32)
        return ((text_dir, loss_sum, temp_sum, bias_sum), image_dir)
    zero = jnp.zeros((), jnp.float32)
    start_carry = (jnp.zeros((total, width), jnp.float32), zero, zero, zero)
    final, image_blocks = lax.scan(step, start_carry, jnp.arange(count, dtype=jnp.int32))
    text_dir, loss_sum, temp_sum, bias_sum = final
    image_dir = image_blocks.reshape(total, width)
    image_grad = back_rows(image_unit, inv_image, image_dir)
    text_grad = back_rows(text_unit, inv_text, text_dir)
    loss = (loss_sum / total).reshape(1)
    temp_grad = (temp_sum / total).reshape(1)
    bias_grad = (bias_sum / total).reshape(1)
    return (loss, image_grad, text_grad, temp_grad, bias_grad)
```

```python
import jax
import jax.numpy as jnp
from jax import lax
from jax.sharding import Mesh
from jax.sharding import PartitionSpec as P

EPS = 1e-06
AXES = ("x", "yh", "z", "yl", "core")
PLANE = ("x", "yh", "yl")
COLUMN = ("z", "core")


def unit_rows(values):
    inverse = lax.rsqrt(jnp.sum(values * values, axis=1, keepdims=True) + EPS)
    return (values * inverse, inverse)


def back_rows(unit, inverse, direction):
    along = jnp.sum(unit * direction, axis=1, keepdims=True)
    return inverse * (direction - unit * along)


def pair_tile(rows_low, row_ids, text_all, text_ids, scale, offset):
    sim = lax.dot_general(
        rows_low, text_all, (((1,), (1,)), ((), ())), preferred_element_type=jnp.float32
    )
    logits = scale * sim + offset
    label = jnp.where(row_ids[:, None] == text_ids[None, :], 1.0, -1.0).astype(jnp.float32)
    loss_sum = jnp.sum(jax.nn.softplus(-label * logits))
    pair_grad = -label * jax.nn.sigmoid(-label * logits)
    temp_sum = jnp.sum(pair_grad * scale * sim)
    bias_sum = jnp.sum(pair_grad)
    pair_low = pair_grad.astype(jnp.bfloat16)
    image_dir = scale * jnp.dot(pair_low, text_all, preferred_element_type=jnp.float32)
    text_term = scale * lax.dot_general(
        pair_low, rows_low, (((0,), (0,)), ((), ())), preferred_element_type=jnp.float32
    )
    return (image_dir, text_term, loss_sum, temp_sum, bias_sum)


def on_device(image_embed, text_embed, log_temp, bias):
    rows = image_embed.shape[0]
    total = rows * 256
    image_unit, inv_image = unit_rows(image_embed)
    text_unit, inv_text = unit_rows(text_embed)
    image_low = image_unit.astype(jnp.bfloat16)
    text_low = text_unit.astype(jnp.bfloat16)
    scale = jnp.exp(log_temp[0])
    offset = bias[0]
    me = lax.axis_index(AXES)
    ids = me * rows + jnp.arange(rows, dtype=jnp.int32)
    text_all = lax.all_gather(text_low, PLANE, axis=0, tiled=True)
    image_all = lax.all_gather(image_low, COLUMN, axis=0, tiled=True)
    x, yh, z, yl, core = (lax.axis_index(a) for a in AXES)
    k = jnp.arange(16 * rows, dtype=jnp.int32)
    blk, off = k // rows, k % rows
    row_ids = ((((x * 2 + yh) * 8 + blk // 2) * 2 + yl) * 2 + blk % 2) * rows + off
    text_ids = (((blk // 2 * 8 + z) * 2 + blk % 2) * 2 + core) * rows + off
    image_dir, text_term, loss_sum, temp_sum, bias_sum = pair_tile(
        image_all, row_ids, text_all, text_ids, scale, offset
    )
    image_dir = lax.psum_scatter(image_dir, COLUMN, scatter_dimension=0, tiled=True)
    text_dir = lax.psum_scatter(text_term, PLANE, scatter_dimension=0, tiled=True)
    sums = lax.psum(jnp.stack([loss_sum, temp_sum, bias_sum]), AXES)
    image_grad = back_rows(image_unit, inv_image, image_dir)
    text_grad = back_rows(text_unit, inv_text, text_dir)
    sums = sums / total
    return (sums[0:1], image_grad, text_grad, sums[1:2], sums[2:3])


def solution(mesh):
    grid = Mesh(mesh.devices.reshape(4, 2, 8, 2, 2), AXES)
    rows = P(AXES, None)
    return jax.shard_map(
        on_device,
        mesh=grid,
        in_specs=(rows, rows, P(), P()),
        out_specs=(P(), rows, rows, P(), P()),
        check_vma=False,
    )
```

```python
import math

import jax
import jax.numpy as jnp
from jax import lax
from jax.experimental import pallas as pl
from jax.experimental.pallas import tpu as pltpu
from jax.sharding import Mesh
from jax.sharding import PartitionSpec as P

EPS = 1e-06
LOG2E = 1.0 / math.log(2.0)
LN2 = math.log(2.0)
AXES = ("x", "yh", "z", "yl", "core")
NX, NY, NZ = 4, 4, 8
ROWS, D = 64, 1152
HALF = ROWS // 2
SIDE = 16 * ROWS
TOTAL = 256 * ROWS
f32, bf16 = jnp.float32, jnp.bfloat16
NSEM = 128


def place():
    x, yh, z, yl, core = (lax.axis_index(a) for a in AXES)
    return x, yh * 2 + yl, z, core


def peer(dx=0, dy=0, dz=0, dc=0):
    x, y, z, core = place()
    y = lax.rem(y + dy, NY)
    return (
        lax.rem(x + dx, NX),
        y // 2,
        lax.rem(z + dz, NZ),
        lax.rem(y, 2),
        lax.rem(core + dc, 2),
    )


PEERS = (
    [dict(dx=d) for d in (1, 2, 3)]
    + [dict(dy=d) for d in (1, 2, 3)]
    + [dict(dz=d) for d in range(1, NZ)]
    + [dict(dc=1)]
)


def fold(v):
    r, c = v.shape
    v = v.reshape(r // 8, 8, c).sum(0)
    return sum(v[:, k * 128 : (k + 1) * 128] for k in range(c // 128))


def pair_terms(sim, scale2, offset2):
    t2 = sim * scale2
    l2 = t2 + offset2
    e = jnp.exp2(l2)
    r = 1.0 / (1.0 + e)
    p = e * r
    small = e * (1.0 - e * (0.5 - e * (1.0 / 3.0 - e * 0.25)))
    sp = jnp.where(e < 0.01, small, jnp.log(1.0 + e))
    return t2, l2, p, r, sp


def dot_nt(a, b):
    return lax.dot_general(a, b, (((1,), (1,)), ((), ())), preferred_element_type=f32)


def dot_tn(a, b):
    return lax.dot_general(a, b, (((0,), (0,)), ((), ())), preferred_element_type=f32)


def rows_at(slot, half=None, count=1):
    if half is None:
        return pl.ds(slot * ROWS, count * ROWS)
    return pl.ds(slot * ROWS + half * HALF, HALF)


def kernel(
    logt_ref, bias_ref, img_ref, txt_ref,
    gimg_ref, gtxt_ref, sums_ref,
    I, T, pair, PI, PT, PTb, SI, XA, YB, QA, QB, RA, RB, ZL, ZR, acc, S,
    ssem, rsem,
):
    barrier = pltpu.get_barrier_semaphore()
    for p in PEERS:
        pl.semaphore_signal(barrier, 1, device_id=peer(**p), device_id_type=pl.DeviceIdType.MESH)

    used = [0]

    def send(src, dst, **to):
        k = used[0]
        used[0] += 1
        c = pltpu.make_async_remote_copy(
            src_ref=src, dst_ref=dst, send_sem=ssem.at[k], recv_sem=rsem.at[k],
            device_id=peer(**to), device_id_type=pl.DeviceIdType.MESH,
        )
        c.start()
        sent.append(c)
        return c

    sent = []

    def inverse(ref):
        v = ref[...]
        return lax.rsqrt(jnp.sum(v * v, axis=1, keepdims=True) + EPS)

    inv_img = inverse(img_ref)
    inv_txt = inverse(txt_ref)
    I[rows_at(0), :] = (img_ref[...] * inv_img).astype(bf16)
    T[rows_at(0), :] = (txt_ref[...] * inv_txt).astype(bf16)
    scale = jnp.exp(jnp.full((8, 128), logt_ref[0], f32))[0:1, 0:1]
    scale2 = scale * LOG2E
    offset2 = jnp.full((1, 1), bias_ref[0] * LOG2E, f32)
    acc[...] = jnp.zeros_like(acc)
    pl.semaphore_wait(barrier, len(PEERS))

    right, left, plane1 = {}, {}, {}
    sib = []

    def ring(step):
        for h in (0, 1):
            if step < 4 or h == 0:
                if step > 1:
                    right[step - 1, h].wait_recv()
                right[step, h] = send(I.at[rows_at(step - 1, h)], I.at[rows_at(step, h)], dz=1)
            if step < 4 or h == 1:
                if step > 1:
                    left[step - 1, h].wait_recv()
                src = (9 - step) % 8
                left[step, h] = send(I.at[rows_at(src, h)], I.at[rows_at(8 - step, h)], dz=7)

    def to_sibling(slot):
        sib.append(send(I.at[rows_at(slot)], I.at[rows_at(8 + slot)], dc=1))

    for d in (1, 3, 2):
        plane1[d, 0] = send(T.at[rows_at(0, 0)], T.at[rows_at(d * 4, 0)], dx=d)
        plane1[d, 1] = send(T.at[rows_at(0, 1)], T.at[rows_at(d, 1)], dy=d)
    ring(1)
    to_sibling(0)
    plane2 = []

    def forward(e):
        for f in (1, 3, 2):
            plane2.append(send(T.at[rows_at(e * 4, 0)], T.at[rows_at(e * 4 + f, 0)], dy=f))
            plane2.append(send(T.at[rows_at(e, 1)], T.at[rows_at(f * 4 + e, 1)], dx=f))

    forward(0)
    ring(2)
    for d in (1, 3, 2):
        plane1[d, 0].wait_recv()
        plane1[d, 1].wait_recv()
        forward(d)
    to_sibling(1)
    to_sibling(7)
    ring(3)
    to_sibling(2)
    to_sibling(6)
    ring(4)
    right[3, 1].wait_recv()
    left[3, 0].wait_recv()
    to_sibling(3)
    to_sibling(5)
    right[4, 0].wait_recv()
    left[4, 1].wait_recv()
    to_sibling(4)
    for c in plane2:
        c.wait_recv()
    for c in sib:
        c.wait_recv()

    CH, RBK = 256, 256

    @pl.loop(0, SIDE // CH)
    def _(j):
        js = pl.ds(pl.multiple_of(j * CH, CH), CH)
        tj = T[js, :]
        for r in range(SIDE // RBK):
            rs = slice(r * RBK, (r + 1) * RBK)
            t2, _, p, _, sp = pair_terms(dot_nt(I[rs, :], tj), scale2, offset2)
            pair[rs, js] = p.astype(bf16)
            acc[0] += fold(sp)
            acc[1] += fold(p)
            acc[2] += fold(p * t2)

    t2, l2, p, r, _ = pair_terms(dot_nt(I[0:ROWS, :], T[0 : 2 * ROWS, :]), scale2, offset2)
    shape = (ROWS, 2 * ROWS)
    same = lax.broadcasted_iota(jnp.int32, shape, 0) == lax.broadcasted_iota(jnp.int32, shape, 1)
    pair[0:ROWS, 0 : 2 * ROWS] = jnp.where(same, -r, p).astype(bf16)
    acc[0] -= fold(jnp.where(same, l2 * LN2, 0.0))
    acc[1] -= fold(jnp.where(same, 1.0, 0.0))
    acc[2] -= fold(jnp.where(same, t2, 0.0))

    mine = place()
    sizes = (NX, NY, NZ, 2)
    names = ("dx", "dy", "dz", "dc")
    stage_copies = {}

    def sums_start(stage, value):
        at = S.at[stage, mine[stage]]
        S[stage, mine[stage]] = value
        stage_copies[stage] = [
            send(at, at, **{names[stage]: d}) for d in range(1, sizes[stage])
        ]

    def sums_next(stage):
        for c in stage_copies[stage]:
            c.wait()
        value = S[stage, 0]
        for k in range(1, sizes[stage]):
            value = value + S[stage, k]
        return value

    row = lax.broadcasted_iota(jnp.int32, (8, 128), 0)
    lanes = [jnp.sum(acc[k], axis=0, keepdims=True) for k in range(3)]
    first = jnp.where(row == 0, lanes[0], jnp.where(row == 1, lanes[1], lanes[2]))
    sums_start(0, first)

    def image_part(base, count, block=256):
        @pl.loop(0, count // block)
        def _(i):
            rs = pl.ds(pl.multiple_of(base + i * block, block), block)
            PI[rs, :] = jnp.dot(pair[rs, :], T[...], preferred_element_type=f32)

    def text_part(dx):
        js = pl.ds(dx * 256, 256)
        v = dot_tn(pair[:, js], I[...])
        PT[js, :] = v
        PTb[js, :] = v.astype(bf16)

    xa, yb = {}, {}

    def plane_send(dx):
        for dy in range(4):
            slot = dx * 4 + dy
            if dx:
                xa[dx, dy] = send(PTb.at[rows_at(slot, 0)], XA.at[dx - 1, dy], dx=(NX - dx))
            if dy:
                yb[dx, dy] = send(PTb.at[rows_at(slot, 1)], YB.at[dy - 1, dx], dy=(NY - dy))

    image_part(512, 512)
    sib2 = [send(PI.at[rows_at(8 + 2 * k, count=2)], SI.at[rows_at(2 * k, count=2)], dc=1) for k in (2, 1, 3, 0)]
    sib2 = {2: sib2[0], 1: sib2[1], 3: sib2[2], 0: sib2[3]}
    text_part(2)
    plane_send(2)
    image_part(256, 256)
    zl, zr = {}, {}

    def chain(dirn, slot, h):
        rs = rows_at(slot, h)
        v = PI[rs, :] + SI[rs, :]
        got = (zl if dirn == "l" else zr).get((slot, h))
        if got is not None:
            got.wait_recv()
            v = v + (ZL if dirn == "l" else ZR)[rs, :]
        PI[rs, :] = v
        if dirn == "l":
            zl[slot - 1, h] = send(PI.at[rs], ZL.at[rows_at(slot - 1, h)], dz=NZ - 1)
        else:
            nxt = (slot + 1) % 8
            zr[nxt, h] = send(PI.at[rs], ZR.at[rows_at(nxt, h)], dz=1)

    sib2[2].wait_recv()
    chain("l", 4, 0)
    chain("r", 4, 1)
    chain("r", 5, 0)
    image_part(0, 256)
    sib2[1].wait_recv()
    chain("l", 3, 1)
    text_part(1)
    plane_send(1)
    sums_start(1, sums_next(0))
    text_part(3)
    plane_send(3)
    chain("l", 3, 0)
    chain("r", 5, 1)
    text_part(0)
    plane_send(0)
    sib2[3].wait_recv()
    chain("l", 2, 1)
    chain("r", 6, 0)
    sums_start(2, sums_next(1))
    chain("l", 2, 0)
    chain("r", 6, 1)
    sib2[0].wait_recv()

    ra, rb = {}, {}

    def second(k):
        va = PT[rows_at(k, 0), :]
        vb = PT[rows_at(k * 4, 1), :]
        for d in (1, 2, 3):
            xa[d, k].wait_recv()
            va = va + XA[d - 1, k].astype(f32)
            yb[k, d].wait_recv()
            vb = vb + YB[d - 1, k].astype(f32)
        QA[k] = va
        QB[k] = vb
        if k:
            ra[k] = send(QA.at[k], RA.at[k - 1], dy=NY - k)
            rb[k] = send(QB.at[k], RB.at[k - 1], dx=NX - k)

    second(2)
    chain("l", 1, 1)
    chain("r", 7, 0)
    second(1)
    sums_start(3, sums_next(2))
    chain("l", 1, 0)
    chain("r", 7, 1)
    second(3)
    second(0)

    total = sums_next(3)
    sums_ref[...] = jnp.broadcast_to(jnp.sum(total, axis=1, keepdims=True), (8, 128))

    def back(ref, inv, direction):
        unit = ref[...] * inv
        along = jnp.sum(unit * direction, axis=1, keepdims=True)
        return inv * (direction - unit * along)

    for k in (1, 3, 2):
        ra[k].wait_recv()
        rb[k].wait_recv()
        QA[0] = QA[0] + RA[k - 1]
        QB[0] = QB[0] + RB[k - 1]
    tdir = jnp.concatenate([QA[0], QB[0]], axis=0) * scale
    gtxt_ref[...] = back(txt_ref, inv_txt, tdir)
    for h in (0, 1):
        zl[0, h].wait_recv()
        zr[0, h].wait_recv()
    own = rows_at(0)
    idir = (PI[own, :] + SI[own, :] + ZL[own, :] + ZR[own, :]) * scale
    gimg_ref[...] = back(img_ref, inv_img, idir)

    done = set()
    for stage in stage_copies:
        done.update(id(c) for c in stage_copies[stage])
    for c in sent:
        if id(c) not in done:
            c.wait_send()


def on_device(image_embed, text_embed, log_temp, bias):
    vmem = pl.BlockSpec(memory_space=pltpu.VMEM)
    smem = pl.BlockSpec(memory_space=pltpu.SMEM)
    grad = jax.ShapeDtypeStruct((ROWS, D), f32)
    gimg, gtxt, sums = pl.pallas_call(
        kernel,
        out_shape=(grad, grad, jax.ShapeDtypeStruct((8, 128), f32)),
        in_specs=[smem, smem, vmem, vmem],
        out_specs=(vmem, vmem, vmem),
        scratch_shapes=[
            pltpu.VMEM((SIDE, D), bf16),
            pltpu.VMEM((SIDE, D), bf16),
            pltpu.VMEM((SIDE, SIDE), bf16),
            pltpu.VMEM((SIDE, D), f32),
            pltpu.VMEM((SIDE, D), f32),
            pltpu.VMEM((SIDE, D), bf16),
            pltpu.VMEM((8 * ROWS, D), f32),
            pltpu.VMEM((3, 4, HALF, D), bf16),
            pltpu.VMEM((3, 4, HALF, D), bf16),
            pltpu.VMEM((4, HALF, D), f32),
            pltpu.VMEM((4, HALF, D), f32),
            pltpu.VMEM((3, HALF, D), f32),
            pltpu.VMEM((3, HALF, D), f32),
            pltpu.VMEM((8 * ROWS, D), f32),
            pltpu.VMEM((8 * ROWS, D), f32),
            pltpu.VMEM((3, 8, 128), f32),
            pltpu.VMEM((4, 8, 8, 128), f32),
            pltpu.SemaphoreType.DMA((NSEM,)),
            pltpu.SemaphoreType.DMA((NSEM,)),
        ],
        compiler_params=pltpu.CompilerParams(
            collective_id=0, has_side_effects=True, vmem_limit_bytes=56 * 2**20
        ),
    )(log_temp, bias, image_embed, text_embed)
    loss = sums[0, 0:1] / TOTAL
    bias_grad = sums[1, 0:1] / TOTAL
    temp_grad = sums[2, 0:1] * (LN2 / TOTAL)
    return (loss, gimg, gtxt, temp_grad, bias_grad)


def solution(mesh):
    grid = Mesh(mesh.devices.reshape(NX, NY // 2, NZ, 2, 2), AXES)
    rows = P(AXES, None)
    return jax.shard_map(
        on_device,
        mesh=grid,
        in_specs=(rows, rows, P(), P()),
        out_specs=(P(), rows, rows, P(), P()),
        check_vma=False,
    )
```

```python
import math

import jax
import jax.numpy as jnp
from jax import lax
from jax.experimental import pallas as pl
from jax.experimental.pallas import tpu as pltpu
from jax.sharding import Mesh
from jax.sharding import PartitionSpec as P

EPS = 1e-06
LOG2E = 1.0 / math.log(2.0)
LN2 = math.log(2.0)
AXES = ("x", "yh", "z", "yl", "core")
NX, NY, NZ = 4, 4, 8
ROWS, D = 64, 1152
HALF = ROWS // 2
QROWS = ROWS // 4
SIDE = 16 * ROWS
QUAD = 4 * ROWS
TOTAL = 256 * ROWS
NARROW_HOPS = 2
NSEM = 160
f32, bf16 = jnp.float32, jnp.bfloat16

IMAGE_AT = {4: 0, 3: 1, 5: 2, 2: 3, 6: 4, 1: 5, 7: 6, 0: 7}
CHUNK_AT = {0: 0, 1: 1, 3: 2, 2: 3}

PEERS = (
    [dict(dx=d) for d in (1, 2, 3)]
    + [dict(dy=d) for d in (1, 2, 3)]
    + [dict(dz=d) for d in range(1, NZ)]
    + [dict(dc=1)]
)


def place():
    x, yh, z, yl, core = (lax.axis_index(a) for a in AXES)
    return x, yh * 2 + yl, z, core


def peer(dx=0, dy=0, dz=0, dc=0):
    x, y, z, core = place()
    y = lax.rem(y + dy, NY)
    return (
        lax.rem(x + dx, NX),
        y // 2,
        lax.rem(z + dz, NZ),
        lax.rem(y, 2),
        lax.rem(core + dc, 2),
    )


def fold(v):
    r, c = v.shape
    v = v.reshape(r // 8, 8, c).sum(0)
    return sum(v[:, k * 128 : (k + 1) * 128] for k in range(c // 128))


def pair_terms(sim, scale2, offset2):
    t2 = sim * scale2
    l2 = t2 + offset2
    e = jnp.exp2(l2)
    r = 1.0 / (1.0 + e)
    p = e * r
    small = e * (1.0 - e * (0.5 - e * (1.0 / 3.0 - e * 0.25)))
    sp = jnp.where(e < 0.01, small, jnp.log(1.0 + e))
    return t2, l2, p, r, sp


def dot_nt(a, b):
    return lax.dot_general(a, b, (((1,), (1,)), ((), ())), preferred_element_type=f32)


def dot_tn(a, b):
    return lax.dot_general(a, b, (((0,), (0,)), ((), ())), preferred_element_type=f32)


def img(slot, half=None, other=0):
    start = other * 8 * ROWS + IMAGE_AT[slot] * ROWS
    if half is None:
        return pl.ds(start, ROWS)
    return pl.ds(start + half * HALF, HALF)


def ta(dx, dy):
    return pl.ds(CHUNK_AT[dx] * QUAD + dy * HALF, HALF)


def tb(dx, dy):
    return pl.ds(CHUNK_AT[dy] * QUAD + QUAD // 2 + dx * HALF, HALF)


def kernel(
    logt_hbm, bias_hbm, img_ref, txt_ref,
    dimg_ref, dtxt_ref, sums_ref,
    logt_ref, bias_ref, I, T, pair, PI, PIb, PT, PTb, SI,
    XA, XB, QA, QB, RA, RB, ZL, ZR, ZLb, ZRb, acc, S,
    lsem, ssem, rsem,
):
    barrier = pltpu.get_barrier_semaphore()
    for p in PEERS:
        pl.semaphore_signal(barrier, 1, device_id=peer(**p), device_id_type=pl.DeviceIdType.MESH)
    fetch = [
        pltpu.make_async_copy(src, dst, lsem.at[k])
        for k, (src, dst) in enumerate(
            ((logt_hbm, logt_ref), (bias_hbm, bias_ref))
        )
    ]
    for c in fetch:
        c.start()

    sent = []

    def send(src, dst, **to):
        k = len(sent)
        c = pltpu.make_async_remote_copy(
            src_ref=src, dst_ref=dst, send_sem=ssem.at[k], recv_sem=rsem.at[k],
            device_id=peer(**to), device_id_type=pl.DeviceIdType.MESH,
        )
        c.start()
        sent.append(c)
        return c

    def unit_low(ref):
        v = ref[...]
        return (v * lax.rsqrt(jnp.sum(v * v, axis=1, keepdims=True) + EPS)).astype(bf16)

    low = unit_low(txt_ref)
    T[ta(0, 0), :] = low[:HALF]
    T[tb(0, 0), :] = low[HALF:]
    I[img(0), :] = unit_low(img_ref)
    pl.semaphore_wait(barrier, len(PEERS))

    right, left, first, near, far, sib = {}, {}, {}, {}, {}, {}

    def quarter(slot, q):
        return pl.ds(IMAGE_AT[slot] * ROWS + q * QROWS, QROWS)

    def ring(step, *quarters):
        for q in quarters:
            if step < 4 or q < 2:
                if step > 1:
                    right[step - 1, q].wait_recv()
                right[step, q] = send(
                    I.at[quarter(step - 1, q)], I.at[quarter(step, q)], dz=1
                )
            if step < 4 or q >= 2:
                if step > 1:
                    left[step - 1, q].wait_recv()
                left[step, q] = send(
                    I.at[quarter((9 - step) % 8, q)], I.at[quarter(8 - step, q)], dz=NZ - 1
                )

    def to_sibling(slot):
        sib[slot] = send(I.at[img(slot)], I.at[img(slot, other=1)], dc=1)

    def forward(e):
        for f in (1, 3) if e != 2 else (2, 1, 3):
            near["a", e, f] = send(T.at[ta(e, 0)], T.at[ta(e, f)], dy=f)
            near["b", e, f] = send(T.at[tb(0, e)], T.at[tb(f, e)], dx=f)

    def forward_far(e):
        f = 1 if e == 0 else 3
        near["a", e, f].wait_recv()
        far["a", e] = send(T.at[ta(e, f)], T.at[ta(e, 2)], dy=f)
        near["b", e, f].wait_recv()
        far["b", e] = send(T.at[tb(f, e)], T.at[tb(2, e)], dx=f)

    def arrived(e):
        if e == 2:
            for f in (1, 3, 2):
                near["a", e, f].wait_recv()
                near["b", e, f].wait_recv()
            return
        f = 3 if e == 0 else 1
        near["a", e, f].wait_recv()
        near["b", e, f].wait_recv()
        far["a", e].wait_recv()
        far["b", e].wait_recv()

    def piece(q, e):
        rs = slice(q * QUAD, (q + 1) * QUAD)
        js = slice(CHUNK_AT[e] * QUAD, (CHUNK_AT[e] + 1) * QUAD)
        t2, _, p, _, sp = pair_terms(dot_nt(I[rs, :], T[js, :]), scale2, offset2)
        pair[rs, js] = p.astype(bf16)
        acc[0] += fold(sp)
        acc[1] += fold(p)
        acc[2] += fold(p * t2)

    def first_send(*ds):
        for d in ds:
            first["a", d] = send(T.at[ta(0, 0)], T.at[ta(d, 0)], dx=d)
            first["b", d] = send(T.at[tb(0, 0)], T.at[tb(0, d)], dy=d)

    def first_wait(d):
        first["a", d].wait_recv()
        first["b", d].wait_recv()

    first_send(1, 3)
    ring(1, 0, 1, 2, 3)
    forward(0)
    first_send(2)
    to_sibling(0)
    for c in fetch:
        c.wait()
    scale2 = jnp.exp(jnp.full((8, 128), logt_ref[0], f32))[0:1, 0:1] * LOG2E
    offset2 = jnp.full((1, 1), bias_ref[0] * LOG2E, f32)
    acc[...] = jnp.zeros_like(acc)
    ring(2, 0, 1)
    first_wait(1)
    forward(1)
    first_wait(3)
    forward(3)
    ring(2, 2, 3)
    to_sibling(1)
    to_sibling(7)
    ring(3, 0)
    forward_far(0)
    first_wait(2)
    forward(2)
    ring(3, 1, 2, 3)
    to_sibling(2)
    to_sibling(6)
    forward_far(1)
    ring(4, 0, 1)
    forward_far(3)
    ring(4, 2, 3)
    arrived(0)
    piece(1, 0)
    for q in (2, 3):
        right[3, q].wait_recv()
        left[3, q - 2].wait_recv()
    to_sibling(3)
    to_sibling(5)
    for k in (0, 1, 7, 2, 6):
        sib[k].wait_recv()
    piece(3, 0)
    for q in (0, 1):
        right[4, q].wait_recv()
        left[4, q + 2].wait_recv()
    to_sibling(4)
    arrived(1)
    piece(1, 1)
    piece(3, 1)
    piece(0, 0)
    piece(0, 1)
    arrived(3)
    piece(1, 3)
    piece(3, 3)
    piece(0, 3)
    arrived(2)
    piece(0, 2)
    piece(1, 2)
    piece(3, 2)
    for k in (3, 5, 4):
        sib[k].wait_recv()
    for e in (0, 1, 3, 2):
        piece(2, e)

    def image_part(q, n=4, first=0):
        start = q * QUAD + first * ROWS
        rs = slice(start, start + n * ROWS)
        PI[rs, :] = jnp.dot(pair[rs, :], T[...], preferred_element_type=f32)

    def text_part(e):
        js = slice(CHUNK_AT[e] * QUAD, (CHUNK_AT[e] + 1) * QUAD)
        v = dot_tn(pair[:, js], I[...])
        if e == 2:
            PTb[js, :] = v.astype(bf16)
        else:
            PT[js, :] = v

    part = {}

    def part_to_sibling(q, n=4, first=0):
        at = q * QUAD + first * ROWS
        part[q, first] = send(
            PI.at[pl.ds(2 * QUAD + at, n * ROWS)], SI.at[pl.ds(at, n * ROWS)], dc=1
        )

    zl, zr = {}, {}

    def chain(way, slot, h):
        hops, got, far_buf, low_buf = (
            (zl, zl.get((slot, h)), ZL, ZLb) if way == "l" else (zr, zr.get((slot, h)), ZR, ZRb)
        )
        rs = img(slot, h)
        v = PI[rs, :] + SI[rs, :]
        hop = 1
        if got is not None:
            copy, hop = got
            copy.wait_recv()
            v = v + (low_buf if hop <= NARROW_HOPS else far_buf)[rs, :].astype(f32)
            hop += 1
        nxt = slot - 1 if way == "l" else (slot + 1) % 8
        to = NZ - 1 if way == "l" else 1
        if hop <= NARROW_HOPS:
            PIb[rs, :] = v.astype(bf16)
            c = send(PIb.at[rs], low_buf.at[img(nxt, h)], dz=to)
        else:
            PI[rs, :] = v
            c = send(PI.at[rs], far_buf.at[img(nxt, h)], dz=to)
        hops[nxt, h] = (c, hop)

    xa, xb = {}, {}

    def plane_first():
        for k in (2, 3, 0, 1):
            way, at = (3, 1) if k % 2 == 0 else (1, 3)
            xa[at, k] = send(PTb.at[ta(2, k)], XA.at[at, k], dx=way)
            xb[at, k] = send(PTb.at[tb(k, 2)], XB.at[at, k], dy=way)

    def plane_next(e, late):
        way, at = (3, 0) if e == 1 else (1, 2)
        for k in (2, 3, 0, 1):
            if ((e, k) in xa) != late:
                continue
            va, vb = PT[ta(e, k), :], PT[tb(k, e), :]
            if late:
                xa[e, k].wait_recv()
                va = va + XA[e, k].astype(f32)
                xb[e, k].wait_recv()
                vb = vb + XB[e, k].astype(f32)
            PTb[ta(e, k), :] = va.astype(bf16)
            xa[at, k] = send(PTb.at[ta(e, k)], XA.at[at, k], dx=way)
            PTb[tb(k, e), :] = vb.astype(bf16)
            xb[at, k] = send(PTb.at[tb(k, e)], XB.at[at, k], dy=way)

    def plane_sum(k):
        for c in (xa[0, k], xa[2, k], xb[0, k], xb[2, k]):
            c.wait_recv()
        QA[k] = PT[ta(0, k), :] + XA[0, k].astype(f32) + XA[2, k].astype(f32)
        QB[k] = PT[tb(k, 0), :] + XB[0, k].astype(f32) + XB[2, k].astype(f32)

    lo, hi = pl.ds(0, HALF // 2), pl.ds(HALF // 2, HALF // 2)
    ra, rb = {}, {}

    def second_far():
        for at, rs, way in ((1, lo, 3), (3, hi, 1)):
            ra[at] = send(QA.at[2, rs], RA.at[at, rs], dy=way)
            rb[at] = send(QB.at[2, rs], RB.at[at, rs], dx=way)

    def second_free(k):
        at, rs, way = (0, hi, 3) if k == 1 else (2, lo, 1)
        ra[at, 0] = send(QA.at[k, rs], RA.at[at, rs], dy=way)
        rb[at, 0] = send(QB.at[k, rs], RB.at[at, rs], dx=way)

    def second_late(k):
        at, rs, way = (0, lo, 3) if k == 1 else (2, hi, 1)
        ra[k].wait_recv()
        QA[k, rs] = QA[k, rs] + RA[k, rs]
        ra[at, 1] = send(QA.at[k, rs], RA.at[at, rs], dy=way)
        rb[k].wait_recv()
        QB[k, rs] = QB[k, rs] + RB[k, rs]
        rb[at, 1] = send(QB.at[k, rs], RB.at[at, rs], dx=way)

    mine = place()
    sizes = (NX, NY, NZ, 2)
    names = ("dx", "dy", "dz", "dc")
    stages = {}

    def sums_start(stage, value):
        S[stage, mine[stage]] = value
        at = S.at[stage, mine[stage]]
        stages[stage] = [send(at, at, **{names[stage]: d}) for d in range(1, sizes[stage])]

    def sums_next(stage):
        for c in stages[stage]:
            c.wait_recv()
        value = S[stage, 0]
        for k in range(1, sizes[stage]):
            value = value + S[stage, k]
        return value

    image_part(2, 2)
    part_to_sibling(0, 2)
    image_part(2, 2, 2)
    part_to_sibling(0, 2, 2)
    text_part(2)
    plane_first()
    image_part(0)
    part[0, 0].wait_recv()
    chain("l", 4, 0)
    chain("r", 4, 1)
    chain("l", 3, 1)
    part[0, 2].wait_recv()
    chain("r", 5, 0)
    text_part(1)
    plane_next(1, False)
    text_part(3)
    plane_next(3, False)

    own, cols = IMAGE_AT[0] * ROWS, CHUNK_AT[0] * QUAD
    t2, l2, p, r, _ = pair_terms(
        dot_nt(I[own : own + ROWS, :], T[cols : cols + QUAD, :]), scale2, offset2
    )
    i = lax.broadcasted_iota(jnp.int32, (ROWS, QUAD), 0)
    j = lax.broadcasted_iota(jnp.int32, (ROWS, QUAD), 1)
    same = j == jnp.where(i < HALF, i, i + (QUAD // 2 - HALF))
    pair[own : own + ROWS, cols : cols + QUAD] = jnp.where(same, -r, p).astype(bf16)
    acc[0] -= fold(jnp.where(same, l2 * LN2, 0.0))
    acc[1] -= fold(jnp.where(same, 1.0, 0.0))
    acc[2] -= fold(jnp.where(same, t2, 0.0))

    row = lax.broadcasted_iota(jnp.int32, (8, 128), 0)
    lanes = [jnp.sum(acc[k], axis=0, keepdims=True) for k in range(3)]
    sums_start(0, jnp.where(row == 0, lanes[0], jnp.where(row == 1, lanes[1], lanes[2])))
    chain("l", 3, 0)
    chain("r", 5, 1)
    image_part(3)
    part_to_sibling(1)
    plane_next(1, True)
    plane_next(3, True)
    chain("l", 2, 1)
    image_part(1)
    part[1, 0].wait_recv()
    chain("r", 6, 0)
    sums_start(1, sums_next(0))
    chain("l", 2, 0)
    chain("r", 6, 1)
    text_part(0)
    chain("l", 1, 1)
    chain("r", 7, 0)
    plane_sum(2)
    second_far()
    sums_start(2, sums_next(1))
    plane_sum(1)
    second_free(1)
    plane_sum(3)
    second_free(3)
    plane_sum(0)
    chain("l", 1, 0)
    chain("r", 7, 1)
    second_late(1)
    second_late(3)
    sums_start(3, sums_next(2))
    total = sums_next(3)
    sums_ref[...] = jnp.broadcast_to(jnp.sum(total, axis=1, keepdims=True), (8, 128))
    for k in (0, 2):
        for n in (0, 1):
            ra[k, n].wait_recv()
            rb[k, n].wait_recv()
    dtxt_ref[:HALF] = QA[0] + (RA[0] + RA[2])
    dtxt_ref[HALF:] = QB[0] + (RB[0] + RB[2])
    for h in (0, 1):
        zl[0, h][0].wait_recv()
        zr[0, h][0].wait_recv()
    rs = img(0)
    dimg_ref[...] = PI[rs, :] + SI[rs, :] + (ZL[rs, :] + ZR[rs, :])
    for c in sent:
        c.wait_send()


def finish(
    logt_ref, sums_ref, img_ref, txt_ref, dimg_ref, dtxt_ref,
    loss_ref, gimg_ref, gtxt_ref, gtemp_ref, gbias_ref,
):
    scale = jnp.exp(logt_ref[...].reshape(1, 1))
    for ref, dref, out in ((img_ref, dimg_ref, gimg_ref), (txt_ref, dtxt_ref, gtxt_ref)):
        v = ref[...]
        inverse = lax.rsqrt(jnp.sum(v * v, axis=1, keepdims=True) + EPS)
        unit = v * inverse
        direction = dref[...] * scale
        along = jnp.sum(unit * direction, axis=1, keepdims=True)
        out[...] = inverse * (direction - unit * along)
    loss_ref[...] = sums_ref[0, 0:1] * (1.0 / TOTAL)
    gbias_ref[...] = sums_ref[1, 0:1] * (1.0 / TOTAL)
    gtemp_ref[...] = sums_ref[2, 0:1] * (LN2 / TOTAL)


def on_device(image_embed, text_embed, log_temp, bias):
    vmem = pl.BlockSpec(memory_space=pltpu.VMEM)
    hbm = pl.BlockSpec(memory_space=pltpu.HBM)
    grad = jax.ShapeDtypeStruct((ROWS, D), f32)
    one = jax.ShapeDtypeStruct((1,), f32)
    half = (HALF, D)
    dimg, dtxt, sums = pl.pallas_call(
        kernel,
        out_shape=(grad, grad, jax.ShapeDtypeStruct((8, 128), f32)),
        in_specs=[hbm, hbm, vmem, vmem],
        out_specs=(vmem,) * 3,
        scratch_shapes=[
            pltpu.SMEM((1,), f32),
            pltpu.SMEM((1,), f32),
            pltpu.VMEM((SIDE, D), bf16),
            pltpu.VMEM((SIDE, D), bf16),
            pltpu.VMEM((SIDE, SIDE), bf16),
            pltpu.VMEM((SIDE, D), f32),
            pltpu.VMEM((8 * ROWS, D), bf16),
            pltpu.VMEM((SIDE, D), f32),
            pltpu.VMEM((SIDE, D), bf16),
            pltpu.VMEM((8 * ROWS, D), f32),
            pltpu.VMEM((4, 4) + half, bf16),
            pltpu.VMEM((4, 4) + half, bf16),
            pltpu.VMEM((4,) + half, f32),
            pltpu.VMEM((4,) + half, f32),
            pltpu.VMEM((4,) + half, f32),
            pltpu.VMEM((4,) + half, f32),
            pltpu.VMEM((8 * ROWS, D), f32),
            pltpu.VMEM((8 * ROWS, D), f32),
            pltpu.VMEM((8 * ROWS, D), bf16),
            pltpu.VMEM((8 * ROWS, D), bf16),
            pltpu.VMEM((3, 8, 128), f32),
            pltpu.VMEM((4, 8, 8, 128), f32),
            pltpu.SemaphoreType.DMA((2,)),
            pltpu.SemaphoreType.DMA((NSEM,)),
            pltpu.SemaphoreType.DMA((NSEM,)),
        ],
        compiler_params=pltpu.CompilerParams(
            collective_id=0, has_side_effects=True, vmem_limit_bytes=52 * 2**20
        ),
    )(log_temp, bias, image_embed, text_embed)
    return pl.pallas_call(
        finish,
        out_shape=(one, grad, grad, one, one),
        in_specs=[vmem] * 6,
        out_specs=(vmem,) * 5,
        compiler_params=pltpu.CompilerParams(vmem_limit_bytes=16 * 2**20),
    )(log_temp, sums, image_embed, text_embed, dimg, dtxt)


def solution(mesh):
    grid = Mesh(mesh.devices.reshape(NX, NY // 2, NZ, 2, 2), AXES)
    rows = P(AXES, None)
    return jax.shard_map(
        on_device,
        mesh=grid,
        in_specs=(rows, rows, P(), P()),
        out_specs=(P(), rows, rows, P(), P()),
        check_vma=False,
    )
```

```python
import math

import jax
import jax.numpy as jnp
from jax import lax
from jax.experimental import pallas as pl
from jax.experimental.pallas import tpu as pltpu
from jax.sharding import Mesh
from jax.sharding import PartitionSpec as P

EPS = 1e-06
LOG2E = 1.0 / math.log(2.0)
LN2 = math.log(2.0)
AXES = ("x", "yh", "z", "yl", "core")
NX, NY, NZ = 4, 4, 8
ROWS, D = 64, 1152
HALF = ROWS // 2
QROWS = ROWS // 4
SIDE = 16 * ROWS
QUAD = 4 * ROWS
TOTAL = 256 * ROWS
NARROW_HOPS = {4: 2, 3: 2}
NSEM = 192
f32, bf16 = jnp.float32, jnp.bfloat16

IMAGE_AT = {4: 0, 3: 1, 5: 2, 2: 3, 6: 4, 1: 5, 7: 6, 0: 7}
CHUNK_AT = {0: 0, 1: 1, 3: 2, 2: 3}

PEERS = (
    [dict(dx=d) for d in (1, 2, 3)]
    + [dict(dy=d) for d in (1, 2, 3)]
    + [dict(dz=d) for d in range(1, NZ)]
    + [dict(dc=1)]
)


def place():
    x, yh, z, yl, core = (lax.axis_index(a) for a in AXES)
    return x, yh * 2 + yl, z, core


def peer(dx=0, dy=0, dz=0, dc=0):
    x, y, z, core = place()
    y = lax.rem(y + dy, NY)
    return (
        lax.rem(x + dx, NX),
        y // 2,
        lax.rem(z + dz, NZ),
        lax.rem(y, 2),
        lax.rem(core + dc, 2),
    )


def fold(v):
    r, c = v.shape
    v = v.reshape(r // 8, 8, c).sum(0)
    return sum(v[:, k * 128 : (k + 1) * 128] for k in range(c // 128))


def pair_terms(sim, scale2, offset2):
    t2 = sim * scale2
    l2 = t2 + offset2
    e = jnp.exp2(l2)
    r = 1.0 / (1.0 + e)
    p = e * r
    small = e * (1.0 - e * (0.5 - e * (1.0 / 3.0 - e * 0.25)))
    sp = jnp.where(e < 0.01, small, jnp.log(1.0 + e))
    return t2, l2, p, r, sp


def dot_nt(a, b):
    return lax.dot_general(a, b, (((1,), (1,)), ((), ())), preferred_element_type=f32)


def dot_tn(a, b):
    return lax.dot_general(a, b, (((0,), (0,)), ((), ())), preferred_element_type=f32)


def img(slot, half=None, other=0):
    start = other * 8 * ROWS + IMAGE_AT[slot] * ROWS
    if half is None:
        return pl.ds(start, ROWS)
    return pl.ds(start + half * HALF, HALF)


def ta(dx, dy):
    return pl.ds(CHUNK_AT[dx] * QUAD + dy * HALF, HALF)


def tb(dx, dy):
    return pl.ds(CHUNK_AT[dy] * QUAD + QUAD // 2 + dx * HALF, HALF)


def kernel(
    logt_hbm, bias_hbm, img_ref, txt_ref,
    dimg_ref, dtxt_ref, sums_ref,
    logt_ref, bias_ref, I, T, pair, PI, PIb, PT, PTb, SI,
    XA, XB, QA, QB, RA, RB, ZL, ZR, ZLb, ZRb, acc, S,
    lsem, ssem, rsem,
):
    barrier = pltpu.get_barrier_semaphore()
    for p in PEERS:
        pl.semaphore_signal(barrier, 1, device_id=peer(**p), device_id_type=pl.DeviceIdType.MESH)
    fetch = [
        pltpu.make_async_copy(src, dst, lsem.at[k])
        for k, (src, dst) in enumerate(
            ((logt_hbm, logt_ref), (bias_hbm, bias_ref))
        )
    ]
    for c in fetch:
        c.start()

    sent = []

    def send(src, dst, **to):
        k = len(sent)
        c = pltpu.make_async_remote_copy(
            src_ref=src, dst_ref=dst, send_sem=ssem.at[k], recv_sem=rsem.at[k],
            device_id=peer(**to), device_id_type=pl.DeviceIdType.MESH,
        )
        c.start()
        sent.append(c)
        return c

    def unit_low(ref):
        v = ref[...]
        return (v * lax.rsqrt(jnp.sum(v * v, axis=1, keepdims=True) + EPS)).astype(bf16)

    low = unit_low(txt_ref)
    T[ta(0, 0), :] = low[:HALF]
    T[tb(0, 0), :] = low[HALF:]
    I[img(0), :] = unit_low(img_ref)
    pl.semaphore_wait(barrier, len(PEERS))

    right, left, first, near, far, sib = {}, {}, {}, {}, {}, {}

    def quarter(slot, q):
        return pl.ds(IMAGE_AT[slot] * ROWS + q * QROWS, QROWS)

    def ring(step, *quarters):
        for q in quarters:
            if step < 4 or q < 2:
                if step > 1:
                    right[step - 1, q].wait_recv()
                right[step, q] = send(
                    I.at[quarter(step - 1, q)], I.at[quarter(step, q)], dz=1
                )
            if step < 4 or q >= 2:
                if step > 1:
                    left[step - 1, q].wait_recv()
                left[step, q] = send(
                    I.at[quarter((9 - step) % 8, q)], I.at[quarter(8 - step, q)], dz=NZ - 1
                )

    def to_sibling(slot):
        sib[slot] = send(I.at[img(slot)], I.at[img(slot, other=1)], dc=1)

    def forward(e):
        for f in (1, 3) if e != 2 else (2, 1, 3):
            near["a", e, f] = send(T.at[ta(e, 0)], T.at[ta(e, f)], dy=f)
            near["b", e, f] = send(T.at[tb(0, e)], T.at[tb(f, e)], dx=f)

    def forward_far(e):
        f = 1 if e == 0 else 3
        near["a", e, f].wait_recv()
        far["a", e] = send(T.at[ta(e, f)], T.at[ta(e, 2)], dy=f)
        near["b", e, f].wait_recv()
        far["b", e] = send(T.at[tb(f, e)], T.at[tb(2, e)], dx=f)

    def arrived(e):
        if e == 2:
            for f in (1, 3, 2):
                near["a", e, f].wait_recv()
                near["b", e, f].wait_recv()
            return
        f = 3 if e == 0 else 1
        near["a", e, f].wait_recv()
        near["b", e, f].wait_recv()
        far["a", e].wait_recv()
        far["b", e].wait_recv()

    def piece(q, e):
        rs = slice(q * QUAD, (q + 1) * QUAD)
        js = slice(CHUNK_AT[e] * QUAD, (CHUNK_AT[e] + 1) * QUAD)
        t2, _, p, _, sp = pair_terms(dot_nt(I[rs, :], T[js, :]), scale2, offset2)
        pair[rs, js] = p.astype(bf16)
        acc[0] += fold(sp)
        acc[1] += fold(p)
        acc[2] += fold(p * t2)

    def first_send(*ds):
        for d in ds:
            first["a", d] = send(T.at[ta(0, 0)], T.at[ta(d, 0)], dx=d)
            first["b", d] = send(T.at[tb(0, 0)], T.at[tb(0, d)], dy=d)

    def first_wait(d):
        first["a", d].wait_recv()
        first["b", d].wait_recv()

    first_send(1, 3)
    ring(1, 0, 1, 2, 3)
    forward(0)
    first_send(2)
    to_sibling(0)
    for c in fetch:
        c.wait()
    scale2 = jnp.exp(jnp.full((8, 128), logt_ref[0], f32))[0:1, 0:1] * LOG2E
    offset2 = jnp.full((1, 1), bias_ref[0] * LOG2E, f32)
    acc[...] = jnp.zeros_like(acc)
    ring(2, 0, 1)
    first_wait(1)
    forward(1)
    first_wait(3)
    forward(3)
    ring(2, 2, 3)
    to_sibling(1)
    to_sibling(7)
    ring(3, 0)
    forward_far(0)
    first_wait(2)
    forward(2)
    ring(3, 1, 2, 3)
    to_sibling(2)
    to_sibling(6)
    forward_far(1)
    ring(4, 0, 1)
    forward_far(3)
    ring(4, 2, 3)
    arrived(0)
    piece(1, 0)

    own, cols = IMAGE_AT[0] * ROWS, CHUNK_AT[0] * QUAD
    t2, l2, p, r, _ = pair_terms(
        dot_nt(I[own : own + ROWS, :], T[cols : cols + QUAD, :]), scale2, offset2
    )
    i = lax.broadcasted_iota(jnp.int32, (ROWS, QUAD), 0)
    j = lax.broadcasted_iota(jnp.int32, (ROWS, QUAD), 1)
    same = j == jnp.where(i < HALF, i, i + (QUAD // 2 - HALF))
    pair[own : own + ROWS, cols : cols + QUAD] = jnp.where(same, -r, p).astype(bf16)
    acc[0] -= fold(jnp.where(same, l2 * LN2, 0.0))
    acc[1] -= fold(jnp.where(same, 1.0, 0.0))
    acc[2] -= fold(jnp.where(same, t2, 0.0))

    for q in (2, 3):
        right[3, q].wait_recv()
        left[3, q - 2].wait_recv()
    to_sibling(3)
    to_sibling(5)
    for k in (0, 1, 7, 2, 6):
        sib[k].wait_recv()
    piece(3, 0)
    for q in (0, 1):
        right[4, q].wait_recv()
        left[4, q + 2].wait_recv()
    to_sibling(4)
    arrived(1)
    piece(1, 1)
    piece(3, 1)
    piece(0, 0)
    piece(0, 1)
    arrived(3)
    piece(1, 3)
    piece(3, 3)
    piece(0, 3)
    arrived(2)
    piece(0, 2)
    piece(1, 2)
    piece(3, 2)
    for k in (3, 5, 4):
        sib[k].wait_recv()
    for e in (0, 1, 3, 2):
        piece(2, e)

    def image_part(q, n=4, first=0):
        start = q * QUAD + first * ROWS
        rs = slice(start, start + n * ROWS)
        PI[rs, :] = jnp.dot(pair[rs, :], T[...], preferred_element_type=f32)

    def text_part(e):
        js = slice(CHUNK_AT[e] * QUAD, (CHUNK_AT[e] + 1) * QUAD)
        v = dot_tn(pair[:, js], I[...])
        if e == 2:
            PTb[js, :] = v.astype(bf16)
        else:
            PT[js, :] = v

    part = {}

    def part_to_sibling(q, n=4, first=0):
        at = q * QUAD + first * ROWS
        part[q, first] = send(
            PI.at[pl.ds(2 * QUAD + at, n * ROWS)], SI.at[pl.ds(at, n * ROWS)], dc=1
        )

    zl, zr = {}, {}

    def chain_one(way, slot, q):
        hops, far_buf, low_buf = (zl, ZL, ZLb) if way == "l" else (zr, ZR, ZRb)
        narrow = NARROW_HOPS[4 if (q < 2) == (way == "l") else 3]
        rs = quarter(slot, q)
        v = PI[rs, :] + SI[rs, :]
        hop = 1
        if (slot, q) in hops:
            copy, hop = hops[slot, q]
            copy.wait_recv()
            v = v + (low_buf if hop <= narrow else far_buf)[rs, :].astype(f32)
            hop += 1
        nxt = slot - 1 if way == "l" else (slot + 1) % 8
        to = NZ - 1 if way == "l" else 1
        if hop <= narrow:
            PIb[rs, :] = v.astype(bf16)
            c = send(PIb.at[rs], low_buf.at[quarter(nxt, q)], dz=to)
        else:
            PI[rs, :] = v
            c = send(PI.at[rs], far_buf.at[quarter(nxt, q)], dz=to)
        hops[nxt, q] = (c, hop)

    def chain(distance, half):
        for k in (0, 1):
            chain_one("l", distance, 2 * half + k)
            chain_one("r", 8 - distance, 2 * (1 - half) + k)

    xa, xb = {}, {}

    def plane_first():
        for k in (2, 3, 0, 1):
            way, at = (3, 1) if k % 2 == 0 else (1, 3)
            xa[at, k] = send(PTb.at[ta(2, k)], XA.at[at, k], dx=way)
            xb[at, k] = send(PTb.at[tb(k, 2)], XB.at[at, k], dy=way)

    def plane_next(e, late):
        way, at = (3, 0) if e == 1 else (1, 2)
        for k in (2, 3, 0, 1):
            if ((e, k) in xa) != late:
                continue
            va, vb = PT[ta(e, k), :], PT[tb(k, e), :]
            if late:
                xa[e, k].wait_recv()
                va = va + XA[e, k].astype(f32)
                xb[e, k].wait_recv()
                vb = vb + XB[e, k].astype(f32)
            PTb[ta(e, k), :] = va.astype(bf16)
            xa[at, k] = send(PTb.at[ta(e, k)], XA.at[at, k], dx=way)
            PTb[tb(k, e), :] = vb.astype(bf16)
            xb[at, k] = send(PTb.at[tb(k, e)], XB.at[at, k], dy=way)

    def plane_sum(k):
        for c in (xa[0, k], xa[2, k], xb[0, k], xb[2, k]):
            c.wait_recv()
        QA[k] = PT[ta(0, k), :] + XA[0, k].astype(f32) + XA[2, k].astype(f32)
        QB[k] = PT[tb(k, 0), :] + XB[0, k].astype(f32) + XB[2, k].astype(f32)

    lo, hi = pl.ds(0, HALF // 2), pl.ds(HALF // 2, HALF // 2)
    ra, rb = {}, {}

    def second_far():
        for at, rs, way in ((1, lo, 3), (3, hi, 1)):
            ra[at] = send(QA.at[2, rs], RA.at[at, rs], dy=way)
            rb[at] = send(QB.at[2, rs], RB.at[at, rs], dx=way)

    def second_free(k):
        at, rs, way = (0, hi, 3) if k == 1 else (2, lo, 1)
        ra[at, 0] = send(QA.at[k, rs], RA.at[at, rs], dy=way)
        rb[at, 0] = send(QB.at[k, rs], RB.at[at, rs], dx=way)

    def second_late(k):
        at, rs, way = (0, lo, 3) if k == 1 else (2, hi, 1)
        ra[k].wait_recv()
        QA[k, rs] = QA[k, rs] + RA[k, rs]
        ra[at, 1] = send(QA.at[k, rs], RA.at[at, rs], dy=way)
        rb[k].wait_recv()
        QB[k, rs] = QB[k, rs] + RB[k, rs]
        rb[at, 1] = send(QB.at[k, rs], RB.at[at, rs], dx=way)

    x, y, z, core = place()
    mine = (core, z, x, y)
    sizes = (2, NZ, NX, NY)
    names = ("dc", "dz", "dx", "dy")
    stages = {}

    def sums_start(stage, value):
        S[stage, mine[stage]] = value
        at = S.at[stage, mine[stage]]
        stages[stage] = [send(at, at, **{names[stage]: d}) for d in range(1, sizes[stage])]

    def sums_next(stage):
        for c in stages[stage]:
            c.wait_recv()
        value = S[stage, 0]
        for k in range(1, sizes[stage]):
            value = value + S[stage, k]
        return value

    row = lax.broadcasted_iota(jnp.int32, (8, 128), 0)
    lanes = [jnp.sum(acc[k], axis=0, keepdims=True) for k in range(3)]
    sums_start(0, jnp.where(row == 0, lanes[0], jnp.where(row == 1, lanes[1], lanes[2])))
    image_part(2, 2)
    part_to_sibling(0, 2)
    image_part(2, 2, 2)
    part_to_sibling(0, 2, 2)
    text_part(2)
    sums_start(1, sums_next(0))
    plane_first()
    image_part(0)
    image_part(3)
    part_to_sibling(1)
    part[0, 0].wait_recv()
    chain(4, 0)
    part[0, 2].wait_recv()
    chain(3, 1)
    text_part(1)
    plane_next(1, False)
    image_part(1)
    text_part(3)
    plane_next(3, False)
    chain(3, 0)
    plane_next(1, True)
    plane_next(3, True)
    sums_start(2, sums_next(1))
    text_part(0)
    part[1, 0].wait_recv()
    chain(2, 1)
    chain(2, 0)
    chain(1, 1)
    plane_sum(2)
    second_far()
    sums_start(3, sums_next(2))
    plane_sum(1)
    second_free(1)
    plane_sum(3)
    second_free(3)
    chain(1, 0)
    plane_sum(0)
    second_late(1)
    second_late(3)
    for k in (0, 2):
        for n in (0, 1):
            ra[k, n].wait_recv()
            rb[k, n].wait_recv()
    dtxt_ref[:HALF] = QA[0] + (RA[0] + RA[2])
    dtxt_ref[HALF:] = QB[0] + (RB[0] + RB[2])
    for q in range(4):
        zl[0, q][0].wait_recv()
        zr[0, q][0].wait_recv()
    rs = img(0)
    dimg_ref[...] = PI[rs, :] + SI[rs, :] + (ZL[rs, :] + ZR[rs, :])
    total = sums_next(3)
    sums_ref[...] = jnp.broadcast_to(jnp.sum(total, axis=1, keepdims=True), (8, 128))
    for c in sent:
        c.wait_send()


def finish(
    logt_ref, sums_ref, img_ref, txt_ref, dimg_ref, dtxt_ref,
    loss_ref, gimg_ref, gtxt_ref, gtemp_ref, gbias_ref,
):
    scale = jnp.exp(logt_ref[...].reshape(1, 1))
    for ref, dref, out in ((img_ref, dimg_ref, gimg_ref), (txt_ref, dtxt_ref, gtxt_ref)):
        v = ref[...]
        inverse = lax.rsqrt(jnp.sum(v * v, axis=1, keepdims=True) + EPS)
        unit = v * inverse
        direction = dref[...] * scale
        along = jnp.sum(unit * direction, axis=1, keepdims=True)
        out[...] = inverse * (direction - unit * along)
    loss_ref[...] = sums_ref[0, 0:1] * (1.0 / TOTAL)
    gbias_ref[...] = sums_ref[1, 0:1] * (1.0 / TOTAL)
    gtemp_ref[...] = sums_ref[2, 0:1] * (LN2 / TOTAL)


def on_device(image_embed, text_embed, log_temp, bias):
    vmem = pl.BlockSpec(memory_space=pltpu.VMEM)
    hbm = pl.BlockSpec(memory_space=pltpu.HBM)
    grad = jax.ShapeDtypeStruct((ROWS, D), f32)
    one = jax.ShapeDtypeStruct((1,), f32)
    half = (HALF, D)
    dimg, dtxt, sums = pl.pallas_call(
        kernel,
        out_shape=(grad, grad, jax.ShapeDtypeStruct((8, 128), f32)),
        in_specs=[hbm, hbm, vmem, vmem],
        out_specs=(vmem,) * 3,
        scratch_shapes=[
            pltpu.SMEM((1,), f32),
            pltpu.SMEM((1,), f32),
            pltpu.VMEM((SIDE, D), bf16),
            pltpu.VMEM((SIDE, D), bf16),
            pltpu.VMEM((SIDE, SIDE), bf16),
            pltpu.VMEM((SIDE, D), f32),
            pltpu.VMEM((8 * ROWS, D), bf16),
            pltpu.VMEM((SIDE, D), f32),
            pltpu.VMEM((SIDE, D), bf16),
            pltpu.VMEM((8 * ROWS, D), f32),
            pltpu.VMEM((4, 4) + half, bf16),
            pltpu.VMEM((4, 4) + half, bf16),
            pltpu.VMEM((4,) + half, f32),
            pltpu.VMEM((4,) + half, f32),
            pltpu.VMEM((4,) + half, f32),
            pltpu.VMEM((4,) + half, f32),
            pltpu.VMEM((8 * ROWS, D), f32),
            pltpu.VMEM((8 * ROWS, D), f32),
            pltpu.VMEM((8 * ROWS, D), bf16),
            pltpu.VMEM((8 * ROWS, D), bf16),
            pltpu.VMEM((3, 8, 128), f32),
            pltpu.VMEM((4, 8, 8, 128), f32),
            pltpu.SemaphoreType.DMA((2,)),
            pltpu.SemaphoreType.DMA((NSEM,)),
            pltpu.SemaphoreType.DMA((NSEM,)),
        ],
        compiler_params=pltpu.CompilerParams(
            collective_id=0, has_side_effects=True, vmem_limit_bytes=52 * 2**20
        ),
    )(log_temp, bias, image_embed, text_embed)
    return pl.pallas_call(
        finish,
        out_shape=(one, grad, grad, one, one),
        in_specs=[vmem] * 6,
        out_specs=(vmem,) * 5,
        compiler_params=pltpu.CompilerParams(vmem_limit_bytes=16 * 2**20),
    )(log_temp, sums, image_embed, text_embed, dimg, dtxt)


def solution(mesh):
    grid = Mesh(mesh.devices.reshape(NX, NY // 2, NZ, 2, 2), AXES)
    rows = P(AXES, None)
    return jax.shard_map(
        on_device,
        mesh=grid,
        in_specs=(rows, rows, P(), P()),
        out_specs=(P(), rows, rows, P(), P()),
        check_vma=False,
    )
```

```python
import math

import jax
import jax.numpy as jnp
from jax import lax
from jax.experimental import pallas as pl
from jax.experimental.pallas import tpu as pltpu
from jax.sharding import Mesh
from jax.sharding import PartitionSpec as P

EPS = 1e-06
LOG2E = 1.0 / math.log(2.0)
LN2 = math.log(2.0)
AXES = ("x", "yh", "z", "yl", "core")
NX, NY, NZ = 4, 4, 8
ROWS, D = 64, 1152
HALF = ROWS // 2
QROWS = ROWS // 4
SIDE = 16 * ROWS
QUAD = 4 * ROWS
TOTAL = 256 * ROWS
NARROW_HOPS = {4: 2, 3: 2}
NSEM = 192
f32, bf16 = jnp.float32, jnp.bfloat16

IMAGE_AT = {4: 0, 3: 1, 5: 2, 2: 3, 6: 4, 1: 5, 7: 6, 0: 7}
CHUNK_AT = {0: 0, 1: 1, 3: 2, 2: 3}

PEERS = (
    [dict(dx=d) for d in (1, 2, 3)]
    + [dict(dy=d) for d in (1, 2, 3)]
    + [dict(dz=d) for d in (1, NZ - 1)]
    + [dict(dc=1)]
)


def place():
    x, yh, z, yl, core = (lax.axis_index(a) for a in AXES)
    return x, yh * 2 + yl, z, core


def peer(dx=0, dy=0, dz=0, dc=0):
    x, y, z, core = place()
    y = lax.rem(y + dy, NY)
    return (
        lax.rem(x + dx, NX),
        y // 2,
        lax.rem(z + dz, NZ),
        lax.rem(y, 2),
        lax.rem(core + dc, 2),
    )


def fold(v):
    r, c = v.shape
    v = v.reshape(r // 8, 8, c).sum(0)
    return sum(v[:, k * 128 : (k + 1) * 128] for k in range(c // 128))


def pair_terms(sim, scale2, offset2):
    t2 = sim * scale2
    l2 = t2 + offset2
    e = jnp.exp2(l2)
    r = 1.0 / (1.0 + e)
    p = e * r
    small = e * (1.0 - e * (0.5 - e * (1.0 / 3.0 - e * 0.25)))
    sp = jnp.where(e < 0.01, small, jnp.log(1.0 + e))
    return t2, l2, p, r, sp


def dot_nt(a, b):
    return lax.dot_general(a, b, (((1,), (1,)), ((), ())), preferred_element_type=f32)


def dot_tn(a, b):
    return lax.dot_general(a, b, (((0,), (0,)), ((), ())), preferred_element_type=f32)


def img(slot, half=None, other=0):
    start = other * 8 * ROWS + IMAGE_AT[slot] * ROWS
    if half is None:
        return pl.ds(start, ROWS)
    return pl.ds(start + half * HALF, HALF)


def ta(dx, dy):
    return pl.ds(CHUNK_AT[dx] * QUAD + dy * HALF, HALF)


def tb(dx, dy):
    return pl.ds(CHUNK_AT[dy] * QUAD + QUAD // 2 + dx * HALF, HALF)


def kernel(
    logt_hbm, bias_hbm, img_ref, txt_ref,
    dimg_ref, dtxt_ref, sums_ref,
    logt_ref, bias_ref, I, T, pair, PI, PIb, PT, PTb, SI,
    XA, XB, QA, QB, RA, RB, ZL, ZR, ZLb, ZRb, acc, S,
    lsem, ssem, rsem,
):
    barrier = pltpu.get_barrier_semaphore()
    for p in PEERS:
        pl.semaphore_signal(barrier, 1, device_id=peer(**p), device_id_type=pl.DeviceIdType.MESH)
    fetch = [
        pltpu.make_async_copy(src, dst, lsem.at[k])
        for k, (src, dst) in enumerate(
            ((logt_hbm, logt_ref), (bias_hbm, bias_ref))
        )
    ]
    for c in fetch:
        c.start()

    sent = []

    def send(src, dst, **to):
        k = len(sent)
        c = pltpu.make_async_remote_copy(
            src_ref=src, dst_ref=dst, send_sem=ssem.at[k], recv_sem=rsem.at[k],
            device_id=peer(**to), device_id_type=pl.DeviceIdType.MESH,
        )
        c.start()
        sent.append(c)
        return c

    def unit_low(ref):
        v = ref[...]
        return (v * lax.rsqrt(jnp.sum(v * v, axis=1, keepdims=True) + EPS)).astype(bf16)

    low = unit_low(txt_ref)
    T[ta(0, 0), :] = low[:HALF]
    T[tb(0, 0), :] = low[HALF:]
    I[img(0), :] = unit_low(img_ref)
    pl.semaphore_wait(barrier, len(PEERS))

    right, left, first, near, far, sib = {}, {}, {}, {}, {}, {}

    def quarter(slot, q):
        return pl.ds(IMAGE_AT[slot] * ROWS + q * QROWS, QROWS)

    def ring(step, *quarters):
        for q in quarters:
            if step < 4 or q < 2:
                if step > 1:
                    right[step - 1, q].wait_recv()
                right[step, q] = send(
                    I.at[quarter(step - 1, q)], I.at[quarter(step, q)], dz=1
                )
            if step < 4 or q >= 2:
                if step > 1:
                    left[step - 1, q].wait_recv()
                left[step, q] = send(
                    I.at[quarter((9 - step) % 8, q)], I.at[quarter(8 - step, q)], dz=NZ - 1
                )

    def to_sibling(slot):
        sib[slot] = send(I.at[img(slot)], I.at[img(slot, other=1)], dc=1)

    def forward(e):
        for f in (1, 3) if e != 2 else (2, 1, 3):
            near["a", e, f] = send(T.at[ta(e, 0)], T.at[ta(e, f)], dy=f)
            near["b", e, f] = send(T.at[tb(0, e)], T.at[tb(f, e)], dx=f)

    def forward_far(e):
        f = 1 if e == 0 else 3
        near["a", e, f].wait_recv()
        far["a", e] = send(T.at[ta(e, f)], T.at[ta(e, 2)], dy=f)
        near["b", e, f].wait_recv()
        far["b", e] = send(T.at[tb(f, e)], T.at[tb(2, e)], dx=f)

    def arrived(e):
        if e == 2:
            for f in (1, 3, 2):
                near["a", e, f].wait_recv()
                near["b", e, f].wait_recv()
            return
        f = 3 if e == 0 else 1
        near["a", e, f].wait_recv()
        near["b", e, f].wait_recv()
        far["a", e].wait_recv()
        far["b", e].wait_recv()

    def piece(q, e):
        rs = slice(q * QUAD, (q + 1) * QUAD)
        js = slice(CHUNK_AT[e] * QUAD, (CHUNK_AT[e] + 1) * QUAD)
        t2, _, p, _, sp = pair_terms(dot_nt(I[rs, :], T[js, :]), scale2, offset2)
        pair[rs, js] = p.astype(bf16)
        acc[0] += fold(sp)
        acc[1] += fold(p)
        acc[2] += fold(p * t2)

    def first_send(*ds):
        for d in ds:
            first["a", d] = send(T.at[ta(0, 0)], T.at[ta(d, 0)], dx=d)
            first["b", d] = send(T.at[tb(0, 0)], T.at[tb(0, d)], dy=d)

    def first_wait(d):
        first["a", d].wait_recv()
        first["b", d].wait_recv()

    first_send(1, 3)
    ring(1, 0, 1, 2, 3)
    forward(0)
    first_send(2)
    to_sibling(0)
    for c in fetch:
        c.wait()
    scale2 = jnp.exp(jnp.full((8, 128), logt_ref[0], f32))[0:1, 0:1] * LOG2E
    offset2 = jnp.full((1, 1), bias_ref[0] * LOG2E, f32)
    acc[...] = jnp.zeros_like(acc)
    ring(2, 0, 1)
    first_wait(1)
    forward(1)
    first_wait(3)
    forward(3)
    ring(2, 2, 3)
    to_sibling(1)
    to_sibling(7)
    ring(3, 0)
    forward_far(0)
    first_wait(2)
    forward(2)
    ring(3, 1, 2, 3)
    to_sibling(2)
    to_sibling(6)
    forward_far(1)
    ring(4, 0, 1)
    forward_far(3)
    ring(4, 2, 3)
    arrived(0)
    piece(1, 0)

    own, cols = IMAGE_AT[0] * ROWS, CHUNK_AT[0] * QUAD
    t2, l2, p, r, _ = pair_terms(
        dot_nt(I[own : own + ROWS, :], T[cols : cols + QUAD, :]), scale2, offset2
    )
    i = lax.broadcasted_iota(jnp.int32, (ROWS, QUAD), 0)
    j = lax.broadcasted_iota(jnp.int32, (ROWS, QUAD), 1)
    same = j == jnp.where(i < HALF, i, i + (QUAD // 2 - HALF))
    pair[own : own + ROWS, cols : cols + QUAD] = jnp.where(same, -r, p).astype(bf16)
    acc[0] -= fold(jnp.where(same, l2 * LN2, 0.0))
    acc[1] -= fold(jnp.where(same, 1.0, 0.0))
    acc[2] -= fold(jnp.where(same, t2, 0.0))

    for q in (2, 3):
        right[3, q].wait_recv()
        left[3, q - 2].wait_recv()
    to_sibling(3)
    to_sibling(5)
    for k in (0, 1, 7, 2, 6):
        sib[k].wait_recv()
    piece(3, 0)
    arrived(1)
    piece(1, 1)
    piece(3, 1)
    for q in (0, 1):
        right[4, q].wait_recv()
        left[4, q + 2].wait_recv()
    to_sibling(4)
    piece(0, 0)
    piece(0, 1)
    arrived(3)
    piece(1, 3)
    piece(3, 3)
    piece(0, 3)
    arrived(2)
    piece(0, 2)
    piece(1, 2)
    piece(3, 2)
    for k in (3, 5, 4):
        sib[k].wait_recv()
    for e in (0, 1, 3, 2):
        piece(2, e)

    def image_part(q, n=4, first=0):
        start = q * QUAD + first * ROWS
        rs = slice(start, start + n * ROWS)
        PI[rs, :] = jnp.dot(pair[rs, :], T[...], preferred_element_type=f32)

    def text_part(e):
        js = slice(CHUNK_AT[e] * QUAD, (CHUNK_AT[e] + 1) * QUAD)
        v = dot_tn(pair[:, js], I[...])
        if e == 2:
            PTb[js, :] = v.astype(bf16)
        else:
            PT[js, :] = v

    part = {}

    def part_to_sibling(q, n=4, first=0):
        at = q * QUAD + first * ROWS
        part[q, first] = send(
            PI.at[pl.ds(2 * QUAD + at, n * ROWS)], SI.at[pl.ds(at, n * ROWS)], dc=1
        )

    zl, zr = {}, {}

    def chain_one(way, slot, q):
        hops, far_buf, low_buf = (zl, ZL, ZLb) if way == "l" else (zr, ZR, ZRb)
        narrow = NARROW_HOPS[4 if (q < 2) == (way == "l") else 3]
        rs = quarter(slot, q)
        v = PI[rs, :] + SI[rs, :]
        hop = 1
        if (slot, q) in hops:
            copy, hop = hops[slot, q]
            copy.wait_recv()
            v = v + (low_buf if hop <= narrow else far_buf)[rs, :].astype(f32)
            hop += 1
        nxt = slot - 1 if way == "l" else (slot + 1) % 8
        to = NZ - 1 if way == "l" else 1
        if hop <= narrow:
            PIb[rs, :] = v.astype(bf16)
            c = send(PIb.at[rs], low_buf.at[quarter(nxt, q)], dz=to)
        else:
            PI[rs, :] = v
            c = send(PI.at[rs], far_buf.at[quarter(nxt, q)], dz=to)
        hops[nxt, q] = (c, hop)

    def chain(distance, half):
        for k in (0, 1):
            chain_one("l", distance, 2 * half + k)
            chain_one("r", 8 - distance, 2 * (1 - half) + k)

    xa, xb = {}, {}

    def plane_first():
        for k in (2, 3, 0, 1):
            way, at = (3, 1) if k % 2 == 0 else (1, 3)
            xa[at, k] = send(PTb.at[ta(2, k)], XA.at[at, k], dx=way)
            xb[at, k] = send(PTb.at[tb(k, 2)], XB.at[at, k], dy=way)

    def plane_next(e, late):
        way, at = (3, 0) if e == 1 else (1, 2)
        for k in (2, 3, 0, 1):
            if ((e, k) in xa) != late:
                continue
            va, vb = PT[ta(e, k), :], PT[tb(k, e), :]
            if late:
                xa[e, k].wait_recv()
                va = va + XA[e, k].astype(f32)
                xb[e, k].wait_recv()
                vb = vb + XB[e, k].astype(f32)
            PTb[ta(e, k), :] = va.astype(bf16)
            xa[at, k] = send(PTb.at[ta(e, k)], XA.at[at, k], dx=way)
            PTb[tb(k, e), :] = vb.astype(bf16)
            xb[at, k] = send(PTb.at[tb(k, e)], XB.at[at, k], dy=way)

    def plane_sum(k):
        for c in (xa[0, k], xa[2, k], xb[0, k], xb[2, k]):
            c.wait_recv()
        QA[k] = PT[ta(0, k), :] + XA[0, k].astype(f32) + XA[2, k].astype(f32)
        QB[k] = PT[tb(k, 0), :] + XB[0, k].astype(f32) + XB[2, k].astype(f32)

    lo, hi = pl.ds(0, HALF // 2), pl.ds(HALF // 2, HALF // 2)
    ra, rb = {}, {}

    def second_far():
        for at, rs, way in ((1, lo, 3), (3, hi, 1)):
            ra[at] = send(QA.at[2, rs], RA.at[at, rs], dy=way)
            rb[at] = send(QB.at[2, rs], RB.at[at, rs], dx=way)

    def second_free(k):
        at, rs, way = (0, hi, 3) if k == 1 else (2, lo, 1)
        ra[at, 0] = send(QA.at[k, rs], RA.at[at, rs], dy=way)
        rb[at, 0] = send(QB.at[k, rs], RB.at[at, rs], dx=way)

    def second_late(k):
        at, rs, way = (0, lo, 3) if k == 1 else (2, hi, 1)
        ra[k].wait_recv()
        QA[k, rs] = QA[k, rs] + RA[k, rs]
        ra[at, 1] = send(QA.at[k, rs], RA.at[at, rs], dy=way)
        rb[k].wait_recv()
        QB[k, rs] = QB[k, rs] + RB[k, rs]
        rb[at, 1] = send(QB.at[k, rs], RB.at[at, rs], dx=way)

    x, y, z, core = place()
    mine = (core, z, x, y)
    sizes = (2, NZ, NX, NY)
    names = ("dc", "dz", "dx", "dy")
    stages = {}

    def sums_start(stage, value):
        S[stage, mine[stage]] = value
        at = S.at[stage, mine[stage]]
        stages[stage] = [send(at, at, **{names[stage]: d}) for d in range(1, sizes[stage])]

    def sums_next(stage):
        for c in stages[stage]:
            c.wait_recv()
        value = S[stage, 0]
        for k in range(1, sizes[stage]):
            value = value + S[stage, k]
        return value

    row = lax.broadcasted_iota(jnp.int32, (8, 128), 0)
    lanes = [jnp.sum(acc[k], axis=0, keepdims=True) for k in range(3)]
    sums_start(0, jnp.where(row == 0, lanes[0], jnp.where(row == 1, lanes[1], lanes[2])))
    image_part(2, 2)
    part_to_sibling(0, 2)
    image_part(2, 2, 2)
    part_to_sibling(0, 2, 2)
    text_part(2)
    sums_start(1, sums_next(0))
    plane_first()
    image_part(0)
    part[0, 0].wait_recv()
    chain(4, 0)
    part[0, 2].wait_recv()
    chain(3, 1)
    image_part(3)
    part_to_sibling(1)
    text_part(1)
    plane_next(1, False)
    image_part(1)
    text_part(3)
    plane_next(3, False)
    chain(3, 0)
    plane_next(1, True)
    plane_next(3, True)
    sums_start(2, sums_next(1))
    text_part(0)
    part[1, 0].wait_recv()
    chain(2, 1)
    chain(2, 0)
    plane_sum(2)
    second_far()
    chain(1, 1)
    sums_start(3, sums_next(2))
    plane_sum(1)
    second_free(1)
    plane_sum(3)
    second_free(3)
    chain(1, 0)
    second_late(1)
    second_late(3)
    plane_sum(0)
    for k in (0, 2):
        for n in (0, 1):
            ra[k, n].wait_recv()
            rb[k, n].wait_recv()
    dtxt_ref[:HALF] = QA[0] + (RA[0] + RA[2])
    dtxt_ref[HALF:] = QB[0] + (RB[0] + RB[2])
    for q in range(4):
        zl[0, q][0].wait_recv()
        zr[0, q][0].wait_recv()
    rs = img(0)
    dimg_ref[...] = PI[rs, :] + SI[rs, :] + (ZL[rs, :] + ZR[rs, :])
    total = sums_next(3)
    sums_ref[...] = jnp.broadcast_to(jnp.sum(total, axis=1, keepdims=True), (8, 128))
    for c in sent:
        c.wait_send()


def finish(
    logt_ref, sums_ref, img_ref, txt_ref, dimg_ref, dtxt_ref,
    loss_ref, gimg_ref, gtxt_ref, gtemp_ref, gbias_ref,
):
    scale = jnp.exp(logt_ref[...].reshape(1, 1))
    for ref, dref, out in ((img_ref, dimg_ref, gimg_ref), (txt_ref, dtxt_ref, gtxt_ref)):
        v = ref[...]
        inverse = lax.rsqrt(jnp.sum(v * v, axis=1, keepdims=True) + EPS)
        unit = v * inverse
        direction = dref[...] * scale
        along = jnp.sum(unit * direction, axis=1, keepdims=True)
        out[...] = inverse * (direction - unit * along)
    loss_ref[...] = sums_ref[0, 0:1] * (1.0 / TOTAL)
    gbias_ref[...] = sums_ref[1, 0:1] * (1.0 / TOTAL)
    gtemp_ref[...] = sums_ref[2, 0:1] * (LN2 / TOTAL)


def on_device(image_embed, text_embed, log_temp, bias):
    vmem = pl.BlockSpec(memory_space=pltpu.VMEM)
    hbm = pl.BlockSpec(memory_space=pltpu.HBM)
    grad = jax.ShapeDtypeStruct((ROWS, D), f32)
    one = jax.ShapeDtypeStruct((1,), f32)
    half = (HALF, D)
    dimg, dtxt, sums = pl.pallas_call(
        kernel,
        out_shape=(grad, grad, jax.ShapeDtypeStruct((8, 128), f32)),
        in_specs=[hbm, hbm, vmem, vmem],
        out_specs=(vmem,) * 3,
        scratch_shapes=[
            pltpu.SMEM((1,), f32),
            pltpu.SMEM((1,), f32),
            pltpu.VMEM((SIDE, D), bf16),
            pltpu.VMEM((SIDE, D), bf16),
            pltpu.VMEM((SIDE, SIDE), bf16),
            pltpu.VMEM((SIDE, D), f32),
            pltpu.VMEM((8 * ROWS, D), bf16),
            pltpu.VMEM((SIDE, D), f32),
            pltpu.VMEM((SIDE, D), bf16),
            pltpu.VMEM((8 * ROWS, D), f32),
            pltpu.VMEM((4, 4) + half, bf16),
            pltpu.VMEM((4, 4) + half, bf16),
            pltpu.VMEM((4,) + half, f32),
            pltpu.VMEM((4,) + half, f32),
            pltpu.VMEM((4,) + half, f32),
            pltpu.VMEM((4,) + half, f32),
            pltpu.VMEM((8 * ROWS, D), f32),
            pltpu.VMEM((8 * ROWS, D), f32),
            pltpu.VMEM((8 * ROWS, D), bf16),
            pltpu.VMEM((8 * ROWS, D), bf16),
            pltpu.VMEM((3, 8, 128), f32),
            pltpu.VMEM((4, 8, 8, 128), f32),
            pltpu.SemaphoreType.DMA((2,)),
            pltpu.SemaphoreType.DMA((NSEM,)),
            pltpu.SemaphoreType.DMA((NSEM,)),
        ],
        compiler_params=pltpu.CompilerParams(
            collective_id=0, has_side_effects=True, vmem_limit_bytes=52 * 2**20
        ),
    )(log_temp, bias, image_embed, text_embed)
    return pl.pallas_call(
        finish,
        out_shape=(one, grad, grad, one, one),
        in_specs=[vmem] * 6,
        out_specs=(vmem,) * 5,
        compiler_params=pltpu.CompilerParams(vmem_limit_bytes=16 * 2**20),
    )(log_temp, sums, image_embed, text_embed, dimg, dtxt)


def solution(mesh):
    grid = Mesh(mesh.devices.reshape(NX, NY // 2, NZ, 2, 2), AXES)
    rows = P(AXES, None)
    return jax.shard_map(
        on_device,
        mesh=grid,
        in_specs=(rows, rows, P(), P()),
        out_specs=(P(), rows, rows, P(), P()),
        check_vma=False,
    )
```

```python
import math

import jax
import jax.numpy as jnp
from jax import lax
from jax.experimental import pallas as pl
from jax.experimental.pallas import tpu as pltpu
from jax.sharding import Mesh
from jax.sharding import PartitionSpec as P

EPS = 1e-06
LOG2E = 1.0 / math.log(2.0)
LN2 = math.log(2.0)
AXES = ("x", "yh", "z", "yl", "core")
NX, NY, NZ = 4, 4, 8
ROWS, D = 64, 1152
HALF = ROWS // 2
QROWS = ROWS // 4
SIDE = 16 * ROWS
QUAD = 4 * ROWS
TOTAL = 256 * ROWS
NARROW_HOPS = {4: 2, 3: 2}
NSEM = 192
f32, bf16 = jnp.float32, jnp.bfloat16

IMAGE_AT = {4: 0, 3: 1, 5: 2, 2: 3, 6: 4, 1: 5, 7: 6, 0: 7}
CHUNK_AT = {0: 0, 1: 1, 3: 2, 2: 3}

PEERS = (
    [dict(dx=d) for d in (1, 2, 3)]
    + [dict(dy=d) for d in (1, 2, 3)]
    + [dict(dz=d) for d in (1, NZ - 1)]
    + [dict(dc=1)]
)


def place():
    x, yh, z, yl, core = (lax.axis_index(a) for a in AXES)
    return x, yh * 2 + yl, z, core


def peer(dx=0, dy=0, dz=0, dc=0):
    x, y, z, core = place()
    y = lax.rem(y + dy, NY)
    return (
        lax.rem(x + dx, NX),
        y // 2,
        lax.rem(z + dz, NZ),
        lax.rem(y, 2),
        lax.rem(core + dc, 2),
    )


def fold(v):
    r, c = v.shape
    v = v.reshape(r // 8, 8, c).sum(0)
    return sum(v[:, k * 128 : (k + 1) * 128] for k in range(c // 128))


def pair_terms(sim, scale2, offset2):
    t2 = sim * scale2
    l2 = t2 + offset2
    e = jnp.exp2(l2)
    r = 1.0 / (1.0 + e)
    p = e * r
    small = e * (1.0 - e * (0.5 - e * (1.0 / 3.0 - e * 0.25)))
    sp = jnp.where(e < 0.01, small, jnp.log(1.0 + e))
    return t2, l2, p, r, sp


def dot_nt(a, b):
    return lax.dot_general(a, b, (((1,), (1,)), ((), ())), preferred_element_type=f32)


def dot_tn(a, b):
    return lax.dot_general(a, b, (((0,), (0,)), ((), ())), preferred_element_type=f32)


def img(slot, half=None, other=0):
    start = other * 8 * ROWS + IMAGE_AT[slot] * ROWS
    if half is None:
        return pl.ds(start, ROWS)
    return pl.ds(start + half * HALF, HALF)


def ta(dx, dy):
    return pl.ds(CHUNK_AT[dx] * QUAD + dy * HALF, HALF)


def tb(dx, dy):
    return pl.ds(CHUNK_AT[dy] * QUAD + QUAD // 2 + dx * HALF, HALF)


def kernel(
    logt_hbm, bias_hbm, img_ref, txt_ref,
    dimg_ref, dtxt_ref, sums_ref,
    logt_ref, bias_ref, I, T, pair, PI, PIb, PT, PTb, SI,
    XA, XB, QA, QB, RA, RB, ZL, ZR, ZLb, ZRb, acc, S,
    lsem, ssem, rsem,
):
    barrier = pltpu.get_barrier_semaphore()
    for p in PEERS:
        pl.semaphore_signal(barrier, 1, device_id=peer(**p), device_id_type=pl.DeviceIdType.MESH)
    fetch = [
        pltpu.make_async_copy(src, dst, lsem.at[k])
        for k, (src, dst) in enumerate(
            ((logt_hbm, logt_ref), (bias_hbm, bias_ref))
        )
    ]
    for c in fetch:
        c.start()

    sent = []

    def send(src, dst, **to):
        k = len(sent)
        c = pltpu.make_async_remote_copy(
            src_ref=src, dst_ref=dst, send_sem=ssem.at[k], recv_sem=rsem.at[k],
            device_id=peer(**to), device_id_type=pl.DeviceIdType.MESH,
        )
        c.start()
        sent.append(c)
        return c

    def unit_low(ref):
        v = ref[...]
        return (v * lax.rsqrt(jnp.sum(v * v, axis=1, keepdims=True) + EPS)).astype(bf16)

    low = unit_low(txt_ref)
    T[ta(0, 0), :] = low[:HALF]
    T[tb(0, 0), :] = low[HALF:]
    pl.semaphore_wait(barrier, len(PEERS))

    right, left, first, near, far, sib = {}, {}, {}, {}, {}, {}

    def quarter(slot, q):
        return pl.ds(IMAGE_AT[slot] * ROWS + q * QROWS, QROWS)

    def ring(step, *quarters):
        for q in quarters:
            if step < 4 or q < 2:
                if step > 1:
                    right[step - 1, q].wait_recv()
                right[step, q] = send(
                    I.at[quarter(step - 1, q)], I.at[quarter(step, q)], dz=1
                )
            if step < 4 or q >= 2:
                if step > 1:
                    left[step - 1, q].wait_recv()
                left[step, q] = send(
                    I.at[quarter((9 - step) % 8, q)], I.at[quarter(8 - step, q)], dz=NZ - 1
                )

    def to_sibling(slot):
        sib[slot] = send(I.at[img(slot)], I.at[img(slot, other=1)], dc=1)

    def forward(e):
        for f in (1, 3) if e != 2 else (2, 1, 3):
            near["a", e, f] = send(T.at[ta(e, 0)], T.at[ta(e, f)], dy=f)
            near["b", e, f] = send(T.at[tb(0, e)], T.at[tb(f, e)], dx=f)

    def forward_far(e):
        f = 1 if e == 0 else 3
        near["a", e, f].wait_recv()
        far["a", e] = send(T.at[ta(e, f)], T.at[ta(e, 2)], dy=f)
        near["b", e, f].wait_recv()
        far["b", e] = send(T.at[tb(f, e)], T.at[tb(2, e)], dx=f)

    def arrived(e):
        if e == 2:
            for f in (1, 3, 2):
                near["a", e, f].wait_recv()
                near["b", e, f].wait_recv()
            return
        f = 3 if e == 0 else 1
        near["a", e, f].wait_recv()
        near["b", e, f].wait_recv()
        far["a", e].wait_recv()
        far["b", e].wait_recv()

    def piece(q, e):
        rs = slice(q * QUAD, (q + 1) * QUAD)
        js = slice(CHUNK_AT[e] * QUAD, (CHUNK_AT[e] + 1) * QUAD)
        t2, _, p, _, sp = pair_terms(dot_nt(I[rs, :], T[js, :]), scale2, offset2)
        pair[rs, js] = p.astype(bf16)
        acc[0] += fold(sp)
        acc[1] += fold(p)
        acc[2] += fold(p * t2)

    def first_send(*ds):
        for d in ds:
            first["a", d] = send(T.at[ta(0, 0)], T.at[ta(d, 0)], dx=d)
            first["b", d] = send(T.at[tb(0, 0)], T.at[tb(0, d)], dy=d)

    def first_wait(d):
        first["a", d].wait_recv()
        first["b", d].wait_recv()

    first_send(1, 3)
    I[img(0), :] = unit_low(img_ref)
    ring(1, 0, 1, 2, 3)
    forward(0)
    first_send(2)
    to_sibling(0)
    for c in fetch:
        c.wait()
    scale2 = jnp.exp(jnp.full((8, 128), logt_ref[0], f32))[0:1, 0:1] * LOG2E
    offset2 = jnp.full((1, 1), bias_ref[0] * LOG2E, f32)
    acc[...] = jnp.zeros_like(acc)
    ring(2, 0, 1)
    first_wait(1)
    forward(1)
    first_wait(3)
    forward(3)
    ring(2, 2, 3)
    to_sibling(1)
    to_sibling(7)
    ring(3, 0)
    forward_far(0)
    first_wait(2)
    forward(2)
    ring(3, 1, 2, 3)
    to_sibling(2)
    to_sibling(6)
    forward_far(1)
    ring(4, 0, 1)
    forward_far(3)
    ring(4, 2, 3)
    arrived(0)
    piece(1, 0)

    own, cols = IMAGE_AT[0] * ROWS, CHUNK_AT[0] * QUAD
    t2, l2, p, r, _ = pair_terms(
        dot_nt(I[own : own + ROWS, :], T[cols : cols + QUAD, :]), scale2, offset2
    )
    i = lax.broadcasted_iota(jnp.int32, (ROWS, QUAD), 0)
    j = lax.broadcasted_iota(jnp.int32, (ROWS, QUAD), 1)
    same = j == jnp.where(i < HALF, i, i + (QUAD // 2 - HALF))
    pair[own : own + ROWS, cols : cols + QUAD] = jnp.where(same, -r, p).astype(bf16)
    acc[0] -= fold(jnp.where(same, l2 * LN2, 0.0))
    acc[1] -= fold(jnp.where(same, 1.0, 0.0))
    acc[2] -= fold(jnp.where(same, t2, 0.0))

    for q in (2, 3):
        right[3, q].wait_recv()
        left[3, q - 2].wait_recv()
    to_sibling(3)
    to_sibling(5)
    for k in (0, 1, 7, 2, 6):
        sib[k].wait_recv()
    piece(3, 0)
    arrived(1)
    piece(1, 1)
    piece(3, 1)
    for q in (0, 1):
        right[4, q].wait_recv()
        left[4, q + 2].wait_recv()
    to_sibling(4)
    piece(0, 0)
    piece(0, 1)
    arrived(3)
    piece(1, 3)
    piece(3, 3)
    piece(0, 3)
    arrived(2)
    piece(0, 2)
    piece(1, 2)
    piece(3, 2)
    for k in (3, 5, 4):
        sib[k].wait_recv()
    for e in (0, 1, 3, 2):
        piece(2, e)

    def image_part(q, n=4, first=0):
        start = q * QUAD + first * ROWS
        rs = slice(start, start + n * ROWS)
        PI[rs, :] = jnp.dot(pair[rs, :], T[...], preferred_element_type=f32)

    def text_part(e):
        js = slice(CHUNK_AT[e] * QUAD, (CHUNK_AT[e] + 1) * QUAD)
        v = dot_tn(pair[:, js], I[...])
        if e == 2:
            PTb[js, :] = v.astype(bf16)
        else:
            PT[js, :] = v

    part = {}

    def part_to_sibling(q, n=4, first=0):
        at = q * QUAD + first * ROWS
        part[q, first] = send(
            PI.at[pl.ds(2 * QUAD + at, n * ROWS)], SI.at[pl.ds(at, n * ROWS)], dc=1
        )

    zl, zr = {}, {}

    def chain_one(way, slot, q):
        hops, far_buf, low_buf = (zl, ZL, ZLb) if way == "l" else (zr, ZR, ZRb)
        narrow = NARROW_HOPS[4 if (q < 2) == (way == "l") else 3]
        rs = quarter(slot, q)
        v = PI[rs, :] + SI[rs, :]
        hop = 1
        if (slot, q) in hops:
            copy, hop = hops[slot, q]
            copy.wait_recv()
            v = v + (low_buf if hop <= narrow else far_buf)[rs, :].astype(f32)
            hop += 1
        nxt = slot - 1 if way == "l" else (slot + 1) % 8
        to = NZ - 1 if way == "l" else 1
        if hop <= narrow:
            PIb[rs, :] = v.astype(bf16)
            c = send(PIb.at[rs], low_buf.at[quarter(nxt, q)], dz=to)
        else:
            PI[rs, :] = v
            c = send(PI.at[rs], far_buf.at[quarter(nxt, q)], dz=to)
        hops[nxt, q] = (c, hop)

    def chain(distance, half):
        for k in (0, 1):
            chain_one("l", distance, 2 * half + k)
            chain_one("r", 8 - distance, 2 * (1 - half) + k)

    xa, xb = {}, {}

    def plane_first():
        for k in (2, 3, 0, 1):
            way, at = (3, 1) if k % 2 == 0 else (1, 3)
            xa[at, k] = send(PTb.at[ta(2, k)], XA.at[at, k], dx=way)
            xb[at, k] = send(PTb.at[tb(k, 2)], XB.at[at, k], dy=way)

    def plane_next(e, late):
        way, at = (3, 0) if e == 1 else (1, 2)
        for k in (2, 3, 0, 1):
            if ((e, k) in xa) != late:
                continue
            va, vb = PT[ta(e, k), :], PT[tb(k, e), :]
            if late:
                xa[e, k].wait_recv()
                va = va + XA[e, k].astype(f32)
                xb[e, k].wait_recv()
                vb = vb + XB[e, k].astype(f32)
            PTb[ta(e, k), :] = va.astype(bf16)
            xa[at, k] = send(PTb.at[ta(e, k)], XA.at[at, k], dx=way)
            PTb[tb(k, e), :] = vb.astype(bf16)
            xb[at, k] = send(PTb.at[tb(k, e)], XB.at[at, k], dy=way)

    def plane_sum(k):
        for c in (xa[0, k], xa[2, k], xb[0, k], xb[2, k]):
            c.wait_recv()
        QA[k] = PT[ta(0, k), :] + XA[0, k].astype(f32) + XA[2, k].astype(f32)
        QB[k] = PT[tb(k, 0), :] + XB[0, k].astype(f32) + XB[2, k].astype(f32)

    lo, hi = pl.ds(0, HALF // 2), pl.ds(HALF // 2, HALF // 2)
    ra, rb = {}, {}

    def second_far():
        for at, rs, way in ((1, lo, 3), (3, hi, 1)):
            ra[at] = send(QA.at[2, rs], RA.at[at, rs], dy=way)
            rb[at] = send(QB.at[2, rs], RB.at[at, rs], dx=way)

    def second_free(k):
        at, rs, way = (0, hi, 3) if k == 1 else (2, lo, 1)
        ra[at, 0] = send(QA.at[k, rs], RA.at[at, rs], dy=way)
        rb[at, 0] = send(QB.at[k, rs], RB.at[at, rs], dx=way)

    def second_late(k):
        at, rs, way = (0, lo, 3) if k == 1 else (2, hi, 1)
        ra[k].wait_recv()
        QA[k, rs] = QA[k, rs] + RA[k, rs]
        ra[at, 1] = send(QA.at[k, rs], RA.at[at, rs], dy=way)
        rb[k].wait_recv()
        QB[k, rs] = QB[k, rs] + RB[k, rs]
        rb[at, 1] = send(QB.at[k, rs], RB.at[at, rs], dx=way)

    x, y, z, core = place()
    mine = (core, z, x, y)
    sizes = (2, NZ, NX, NY)
    names = ("dc", "dz", "dx", "dy")
    stages = {}

    def sums_start(stage, value):
        S[stage, mine[stage]] = value
        at = S.at[stage, mine[stage]]
        stages[stage] = [send(at, at, **{names[stage]: d}) for d in range(1, sizes[stage])]

    def sums_next(stage):
        for c in stages[stage]:
            c.wait_recv()
        value = S[stage, 0]
        for k in range(1, sizes[stage]):
            value = value + S[stage, k]
        return value

    row = lax.broadcasted_iota(jnp.int32, (8, 128), 0)
    lanes = [jnp.sum(acc[k], axis=0, keepdims=True) for k in range(3)]
    sums_start(0, jnp.where(row == 0, lanes[0], jnp.where(row == 1, lanes[1], lanes[2])))
    image_part(2, 2)
    part_to_sibling(0, 2)
    image_part(2, 2, 2)
    part_to_sibling(0, 2, 2)
    text_part(2)
    sums_start(1, sums_next(0))
    plane_first()
    image_part(0)
    part[0, 0].wait_recv()
    chain(4, 0)
    part[0, 2].wait_recv()
    chain(3, 1)
    image_part(3)
    part_to_sibling(1)
    text_part(1)
    plane_next(1, False)
    image_part(1)
    text_part(3)
    plane_next(3, False)
    chain(3, 0)
    plane_next(1, True)
    plane_next(3, True)
    sums_start(2, sums_next(1))
    text_part(0)
    part[1, 0].wait_recv()
    chain(2, 1)
    chain(2, 0)
    plane_sum(2)
    second_far()
    chain(1, 1)
    sums_start(3, sums_next(2))
    plane_sum(1)
    second_free(1)
    plane_sum(3)
    second_free(3)
    chain(1, 0)
    second_late(1)
    second_late(3)
    plane_sum(0)
    for k in (0, 2):
        for n in (0, 1):
            ra[k, n].wait_recv()
            rb[k, n].wait_recv()
    dtxt_ref[:HALF] = QA[0] + (RA[0] + RA[2])
    dtxt_ref[HALF:] = QB[0] + (RB[0] + RB[2])
    for q in range(4):
        zl[0, q][0].wait_recv()
        zr[0, q][0].wait_recv()
    rs = img(0)
    dimg_ref[...] = PI[rs, :] + SI[rs, :] + (ZL[rs, :] + ZR[rs, :])
    total = sums_next(3)
    sums_ref[...] = jnp.broadcast_to(jnp.sum(total, axis=1, keepdims=True), (8, 128))
    for c in sent:
        c.wait_send()


def finish(
    logt_ref, sums_ref, img_ref, txt_ref, dimg_ref, dtxt_ref,
    loss_ref, gimg_ref, gtxt_ref, gtemp_ref, gbias_ref,
):
    scale = jnp.exp(logt_ref[...].reshape(1, 1))
    for ref, dref, out in ((img_ref, dimg_ref, gimg_ref), (txt_ref, dtxt_ref, gtxt_ref)):
        v = ref[...]
        inverse = lax.rsqrt(jnp.sum(v * v, axis=1, keepdims=True) + EPS)
        unit = v * inverse
        direction = dref[...] * scale
        along = jnp.sum(unit * direction, axis=1, keepdims=True)
        out[...] = inverse * (direction - unit * along)
    loss_ref[...] = sums_ref[0, 0:1] * (1.0 / TOTAL)
    gbias_ref[...] = sums_ref[1, 0:1] * (1.0 / TOTAL)
    gtemp_ref[...] = sums_ref[2, 0:1] * (LN2 / TOTAL)


def on_device(image_embed, text_embed, log_temp, bias):
    vmem = pl.BlockSpec(memory_space=pltpu.VMEM)
    hbm = pl.BlockSpec(memory_space=pltpu.HBM)
    grad = jax.ShapeDtypeStruct((ROWS, D), f32)
    one = jax.ShapeDtypeStruct((1,), f32)
    half = (HALF, D)
    dimg, dtxt, sums = pl.pallas_call(
        kernel,
        out_shape=(grad, grad, jax.ShapeDtypeStruct((8, 128), f32)),
        in_specs=[hbm, hbm, vmem, vmem],
        out_specs=(vmem,) * 3,
        scratch_shapes=[
            pltpu.SMEM((1,), f32),
            pltpu.SMEM((1,), f32),
            pltpu.VMEM((SIDE, D), bf16),
            pltpu.VMEM((SIDE, D), bf16),
            pltpu.VMEM((SIDE, SIDE), bf16),
            pltpu.VMEM((SIDE, D), f32),
            pltpu.VMEM((8 * ROWS, D), bf16),
            pltpu.VMEM((SIDE, D), f32),
            pltpu.VMEM((SIDE, D), bf16),
            pltpu.VMEM((8 * ROWS, D), f32),
            pltpu.VMEM((4, 4) + half, bf16),
            pltpu.VMEM((4, 4) + half, bf16),
            pltpu.VMEM((4,) + half, f32),
            pltpu.VMEM((4,) + half, f32),
            pltpu.VMEM((4,) + half, f32),
            pltpu.VMEM((4,) + half, f32),
            pltpu.VMEM((8 * ROWS, D), f32),
            pltpu.VMEM((8 * ROWS, D), f32),
            pltpu.VMEM((8 * ROWS, D), bf16),
            pltpu.VMEM((8 * ROWS, D), bf16),
            pltpu.VMEM((3, 8, 128), f32),
            pltpu.VMEM((4, 8, 8, 128), f32),
            pltpu.SemaphoreType.DMA((2,)),
            pltpu.SemaphoreType.DMA((NSEM,)),
            pltpu.SemaphoreType.DMA((NSEM,)),
        ],
        compiler_params=pltpu.CompilerParams(
            collective_id=0, has_side_effects=True, vmem_limit_bytes=52 * 2**20
        ),
    )(log_temp, bias, image_embed, text_embed)
    return pl.pallas_call(
        finish,
        out_shape=(one, grad, grad, one, one),
        in_specs=[vmem] * 6,
        out_specs=(vmem,) * 5,
        compiler_params=pltpu.CompilerParams(vmem_limit_bytes=16 * 2**20),
    )(log_temp, sums, image_embed, text_embed, dimg, dtxt)


def solution(mesh):
    grid = Mesh(mesh.devices.reshape(NX, NY // 2, NZ, 2, 2), AXES)
    rows = P(AXES, None)
    return jax.shard_map(
        on_device,
        mesh=grid,
        in_specs=(rows, rows, P(), P()),
        out_specs=(P(), rows, rows, P(), P()),
        check_vma=False,
    )
```
